128 devices in a mesh: rep: 16 (over x_lo, y, core), shard: 8 (over z, x_hi).
Axes of the slice: x: 4 (x_hi: 2, x_lo: 2; x = x_hi * 2 + x_lo), y: 4, z: 4, core: 2. Of those that a mesh axis runs over, the one named last changes fastest.
Arguments:
- block_input: bfloat16 [16, 1024, 1024], P('rep', 'shard'), may hold values from -6 to 6
- attn_gain: bfloat16 [1024], P('shard'), may hold values from 0.5 to 1.5
- attn_bias: bfloat16 [1024], P('shard'), may hold values from -4 to 4
- query_key_value_weight: bfloat16 [1024, 3072], P('shard'), may hold values from -0.1875 to 0.1875
- query_key_value_bias: bfloat16 [3072], P('shard'), may hold values from -6 to 6
- output_projection_weight: bfloat16 [1024, 1024], P('shard'), may hold values from -0.75 to 0.75
- mlp_gain: bfloat16 [1024], P('shard'), may hold values from 0.5 to 1.5
- mlp_bias: bfloat16 [1024], P('shard'), may hold values from -4 to 4
- gate_up_projection_weight: bfloat16 [1024, 5632], P('shard'), may hold values from -0.1875 to 0.1875
- down_projection_weight: bfloat16 [2816, 1024], P('shard'), may hold values from -0.109375 to 0.109375
- out_grad: bfloat16 [16, 1024, 1024], P('rep', 'shard'), may hold values from -6 to 6
Outputs:
- block_output: bfloat16 [16, 1024, 1024], P('rep', 'shard')
- input_grad: bfloat16 [16, 1024, 1024], P('rep', 'shard')
- attn_gain_grad: float32 [1024], P('shard')
- attn_bias_grad: float32 [1024], P('shard')
- qkv_weight_grad: float32 [1024, 3072], P('shard')
- qkv_bias_grad: float32 [3072], P('shard')
- out_weight_grad: float32 [1024, 1024], P('shard')
- mlp_gain_grad: float32 [1024], P('shard')
- mlp_bias_grad: float32 [1024], P('shard')
- gate_up_weight_grad: float32 [1024, 5632], P('shard')
- down_weight_grad: float32 [2816, 1024], P('shard')
The draws below stay inside these ranges and needn't reach their ends.
All inputs are finite; a program needn't handle non-finite values.
Results may differ from the reference program's by a relative error of at most 0.025.
Values may be sent and summed in bfloat16 or wider, within the bound.
No kernel may reach another device: no remote copies, remote signals or barrier semaphores. Data moves between devices by JAX's collectives and lax.ppermute only.
A program may use at most 128 MiB of HBM per device.

```python
import jax
import jax.numpy as jnp
from jax import lax

D = 1024
HEADS = 16
HEAD_DIM = 64
FF = 2816
ROTARY = 16
SEQ_LEN = 1024
SEQUENCES = 16


def block_levels(rng, dims, cuts, least, top_value):
    def one(dim, blocks):
        heights = jax.random.uniform(jax.random.fold_in(jax.random.fold_in(rng, 6), dim), (blocks,), jnp.float32, least / len(cuts), top_value / len(cuts))
        return jnp.repeat(jnp.exp(heights), dims[dim] // blocks).reshape((-1,) + (1,) * (len(dims) - dim - 1))

    level = one(*cuts[0])
    for cut in cuts[1:]:
        level = level * one(*cut)
    return level


def bell_draw(key, shape, scale, bound, shards=(), kind=jnp.bfloat16):
    factor_of = block_levels(key, shape, shards, -0.22, 0.18) if shards else 1.0
    entries = jax.random.normal(key, shape, jnp.float32) * scale * factor_of
    return jnp.minimum(jnp.maximum(entries, -bound), bound).astype(kind)


def setup_inputs(seed: int = 0) -> dict:
    key_of = jax.random.split(jax.random.key(seed), 12)
    return {
        "block_input": bell_draw(key_of[0], (SEQUENCES, SEQ_LEN, D), 1.0, 6.0, ((0, 16), (1, 8))),
        "attn_gain": jnp.clip(1.0 + 0.1 * jax.random.normal(key_of[1], (D,), jnp.float32), 0.5, 1.5).astype(jnp.bfloat16),
        "attn_bias": bell_draw(key_of[2], (D,), 0.3, 4.0, ((0, 8),)),
        "query_key_value_weight": bell_draw(key_of[3], (D, 3 * D), D ** -0.5, 0.1875, ((0, 8),)),
        "query_key_value_bias": bell_draw(key_of[4], (3 * D,), 0.5, 6.0, ((0, 8),)),
        "output_projection_weight": bell_draw(key_of[5], (D, D), (D // 16) ** -0.5, 0.75, ((0, 8),)),
        "mlp_gain": jnp.clip(1.0 + 0.1 * jax.random.normal(key_of[6], (D,), jnp.float32), 0.5, 1.5).astype(jnp.bfloat16),
        "mlp_bias": bell_draw(key_of[7], (D,), 0.3, 4.0, ((0, 8),)),
        "gate_up_projection_weight": bell_draw(key_of[8], (D, 2 * FF), D ** -0.5, 0.1875, ((0, 8),)),
        "down_projection_weight": bell_draw(key_of[9], (FF, D), FF ** -0.5, 0.109375, ((0, 8),)),
        "out_grad": bell_draw(key_of[10], (SEQUENCES, SEQ_LEN, D), 1.0, 6.0, ((0, 16), (1, 8))),
    }


EPSILON = 1e-05
SCORE_SCALE = 0.125
PRECISION_FULL = lax.Precision.HIGHEST

@jax.custom_vjp
def low(v):
    return lax.optimization_barrier(v.astype(jnp.bfloat16)).astype(jnp.float32)

@jax.custom_vjp
def low_back(v):
    return v

def low_keep(v):
    return (low(v), None)

def low_pass(kept, grad):
    return (grad,)

def back_keep(v):
    return (v, None)

def back_low(kept, grad):
    return (low(grad),)
low.defvjp(low_keep, low_pass)
low_back.defvjp(back_keep, back_low)

def normalize(values):
    center = values - lax.optimization_barrier(jnp.mean(values, axis=-1, keepdims=True))
    variance = lax.optimization_barrier(jnp.mean(center * center, axis=-1, keepdims=True))
    inverse = lax.rsqrt(variance + EPSILON)
    return center * inverse

def rotary_tables(positions, rotary):
    half_rot = rotary // 2
    frequency = 10000.0 ** (-jnp.arange(half_rot, dtype=jnp.float32) * 2.0 / rotary)
    angles = positions.astype(jnp.float32)[:, None] * frequency[None, :]
    return (jnp.cos(angles)[:, None, :], jnp.sin(angles)[:, None, :])

def rotate(heads_val, cosine, sine_table, rotary, direction):
    half_rot = rotary // 2
    lead_part = heads_val[..., :half_rot]
    second = heads_val[..., half_rot:rotary]
    new_lead = lead_part * cosine - direction * second * sine_table
    new_second = second * cosine + direction * lead_part * sine_table
    return jnp.concatenate([new_lead, new_second, heads_val[..., rotary:]], axis=-1)

def attend(packed):
    queries, key_rows, value_rows = packed
    positions = jnp.arange(SEQ_LEN)
    scores = jnp.einsum('qhd,khd->hqk', queries, key_rows, precision=PRECISION_FULL) * SCORE_SCALE
    scores = low_back(scores)
    visible = positions[None, None, :] <= positions[None, :, None]
    scores = jnp.where(visible, scores, -jnp.inf)
    row_max = lax.optimization_barrier(jnp.max(scores, axis=-1, keepdims=True))
    exp_scores = jnp.exp(scores - row_max)
    shares = exp_scores / lax.optimization_barrier(jnp.sum(exp_scores, axis=-1, keepdims=True))
    return jnp.einsum('hqk,khd->qhd', low(shares), value_rows, precision=PRECISION_FULL)

def forward(transformer_block, attn_gain, attn_bias, query_key_value_weight, query_key_value_bias, output_projection_weight, mlp_gain, mlp_bias, gate_up_projection_weight, down_projection_weight):
    seq_total = transformer_block.shape[0]
    first_input = low(normalize(transformer_block) * attn_gain + attn_bias)
    query_key_value = low_back(jnp.einsum('wfa,ao->wfo', first_input, query_key_value_weight, precision=PRECISION_FULL) + query_key_value_bias)
    shape_four = (seq_total, SEQ_LEN, HEADS, HEAD_DIM)
    cosine, sine_table = rotary_tables(jnp.arange(SEQ_LEN), ROTARY)
    queries = low(rotate(query_key_value[..., :D].reshape(shape_four), cosine, sine_table, ROTARY, 1.0))
    key_rows = low(rotate(query_key_value[..., D:2 * D].reshape(shape_four), cosine, sine_table, ROTARY, 1.0))
    value_rows = low(query_key_value[..., 2 * D:].reshape(shape_four))
    attention_output = lax.map(jax.checkpoint(attend), (queries, key_rows, value_rows))
    attention_output = low_back(low(attention_output.reshape(seq_total, SEQ_LEN, D)))
    mixed_output = transformer_block + low_back(jnp.einsum('wfa,ao->wfo', attention_output, output_projection_weight, precision=PRECISION_FULL))
    second_input = low(normalize(mixed_output) * mlp_gain + mlp_bias)
    gate_up_product = low_back(jnp.einsum('wfa,ao->wfo', second_input, gate_up_projection_weight, precision=PRECISION_FULL))
    hidden_state = low(jax.nn.silu(gate_up_product[..., :FF]) * gate_up_product[..., FF:])
    return mixed_output + low_back(jnp.einsum('knu,ua->kna', hidden_state, down_projection_weight, precision=PRECISION_FULL))

def reference(block_input, attn_gain, attn_bias, query_key_value_weight, query_key_value_bias, output_projection_weight, mlp_gain, mlp_bias, gate_up_projection_weight, down_projection_weight, out_grad):
    params = [arg.astype(jnp.float32) for arg in (block_input, attn_gain, attn_bias, query_key_value_weight, query_key_value_bias, output_projection_weight, mlp_gain, mlp_bias, gate_up_projection_weight, down_projection_weight)]
    result, pullback = jax.vjp(forward, *params)
    grads = pullback(out_grad.astype(jnp.float32))
    return (result.astype(jnp.bfloat16), grads[0].astype(jnp.bfloat16), grads[1], grads[2], grads[3], grads[4], grads[5], grads[6], grads[7], grads[8], grads[9])
```

```python
import jax
import jax.numpy as jnp
import numpy as np
from jax import lax
from jax.experimental import pallas as pl
from jax.experimental.pallas import tpu as pltpu
from jax.sharding import PartitionSpec as P

D = 1024
HEADS = 16
HEAD_DIM = 64
FF = 2816
ROTARY = 16
SEQ = 1024

EPSILON = 1e-05
SCORE_SCALE = 0.125

SHARD = ("z", "xh")
F32 = jnp.float32
BF16 = jnp.bfloat16


def normalize(values):
    center = values - jnp.mean(values, axis=-1, keepdims=True)
    variance = jnp.mean(center * center, axis=-1, keepdims=True)
    inverse = lax.rsqrt(variance + EPSILON)
    return (center * inverse, inverse)


def norm_back(scaled_grad, normed, inverse):
    return inverse * (
        scaled_grad
        - jnp.mean(scaled_grad, axis=-1, keepdims=True)
        - normed * jnp.mean(scaled_grad * normed, axis=-1, keepdims=True)
    )


def rotary_tables():
    half = ROTARY // 2
    frequency = np.float32(10000.0) ** (-np.arange(half, dtype=np.float32) * np.float32(2.0) / np.float32(ROTARY))
    angles = np.arange(SEQ, dtype=np.float32)[None, :] * frequency.astype(np.float32)[:, None]
    return np.cos(angles).astype(np.float32), np.sin(angles).astype(np.float32)


def exchange(value, axes):
    return lax.all_to_all(value, axes, 0, 0, tiled=True)


def spread(value, axes, count):
    return exchange(jnp.broadcast_to(value[None], (count,) + value.shape), axes)


def swap(value, axis):
    return lax.ppermute(value, axis, [(0, 1), (1, 0)])


def index_of(xl, y, c, z, xh):
    return (((xl * 4 + y) * 2 + c) * 4 + z) * 2 + xh


def move(value, target):
    pairs = []
    for xl in range(2):
        for y in range(4):
            for c in range(2):
                for z in range(4):
                    for xh in range(2):
                        pairs.append((index_of(xl, y, c, z, xh), index_of(*target(xl, y, c, z, xh))))
    return lax.ppermute(value, ("xl", "y", "c", "z", "xh"), pairs)


def dot(a, b, dims):
    return lax.dot_general(a, b, (dims, ((), ())), preferred_element_type=F32)


BLOCK = 256


def attend_kernel(qkv_ref, bias_ref, cos_ref, sin_ref, out_qkv_ref, attended_ref, lse_ref):
    cos = cos_ref[...]
    sin = sin_ref[...]
    for kind in range(3):
        for head in range(2):
            base = kind * 128 + head * 64
            full = qkv_ref[base : base + 64, :] + bias_ref[base : base + 64, :]
            if kind < 2:
                a = full[0:8]
                b = full[8:16]
                full = jnp.concatenate([a * cos - b * sin, b * cos + a * sin, full[16:]], axis=0)
            out_qkv_ref[base : base + 64, :] = full.astype(BF16)
    row = lax.broadcasted_iota(jnp.int32, (BLOCK, BLOCK), 0)
    col = lax.broadcasted_iota(jnp.int32, (BLOCK, BLOCK), 1)
    for head in range(2):
        key_t = out_qkv_ref[128 + head * 64 : 128 + head * 64 + 64, :]
        value_t = out_qkv_ref[256 + head * 64 : 256 + head * 64 + 64, :]
        keys = key_t.T
        for block in range(SEQ // BLOCK):
            lo = block * BLOCK
            hi = lo + BLOCK
            query_t = out_qkv_ref[head * 64 : head * 64 + 64, lo:hi] * jnp.bfloat16(SCORE_SCALE)
            parts = []
            if block:
                parts.append(dot(keys[:lo], query_t, ((1,), (0,))))
            diag = dot(keys[lo:hi], query_t, ((1,), (0,)))
            parts.append(jnp.where(row <= col, diag, -jnp.inf))
            scores = jnp.concatenate(parts, axis=0) if block else parts[0]
            top = jnp.max(scores, axis=0, keepdims=True)
            exps = jnp.exp(scores - top)
            total = jnp.sum(exps, axis=0, keepdims=True)
            out_t = dot(value_t[:, :hi], exps.astype(BF16), ((1,), (0,))) / total
            attended_ref[lo:hi, head * 64 : head * 64 + 64] = out_t.T.astype(BF16)
            lse_ref[head : head + 1, lo:hi] = top + jnp.log(total)


def attend_back_kernel(qkv_ref, grad_ref, lse_ref, cos_ref, sin_ref, out_ref, dkey, dvalue):
    cos = cos_ref[...]
    sin = sin_ref[...]
    row = lax.broadcasted_iota(jnp.int32, (BLOCK, BLOCK), 0)
    col = lax.broadcasted_iota(jnp.int32, (BLOCK, BLOCK), 1)

    def turn_back(grad):
        a = grad[0:8]
        b = grad[8:16]
        return jnp.concatenate([a * cos + b * sin, b * cos - a * sin, grad[16:]], axis=0)

    for head in range(2):
        dkey[...] = jnp.zeros_like(dkey)
        dvalue[...] = jnp.zeros_like(dvalue)
        key_t = qkv_ref[128 + head * 64 : 128 + head * 64 + 64, :]
        keys = key_t.T
        values = qkv_ref[256 + head * 64 : 256 + head * 64 + 64, :].T
        dquery = []
        for block in range(SEQ // BLOCK):
            lo = block * BLOCK
            hi = lo + BLOCK
            query_t = qkv_ref[head * 64 : head * 64 + 64, lo:hi] * jnp.bfloat16(SCORE_SCALE)
            query = query_t.T
            grad = grad_ref[lo:hi, head * 64 : head * 64 + 64]
            grad_t = grad.T
            lse = lse_ref[head : head + 1, lo:hi]
            parts = []
            if block:
                parts.append(jnp.exp(dot(keys[:lo], query_t, ((1,), (0,))) - lse))
            diag = jnp.exp(dot(keys[lo:hi], query_t, ((1,), (0,))) - lse)
            parts.append(jnp.where(row <= col, diag, 0.0))
            shares = jnp.concatenate(parts, axis=0) if block else parts[0]
            dshares = dot(values[:hi], grad_t, ((1,), (0,)))
            row_dot = jnp.sum(shares * dshares, axis=0, keepdims=True)
            dscores = (shares * (dshares - row_dot)).astype(BF16)
            dvalue[:hi] += dot(shares.astype(BF16), grad, ((1,), (0,)))
            dkey[:hi] += dot(dscores, query, ((1,), (0,)))
            dquery.append(dot(key_t[:, :hi], dscores, ((1,), (0,))) * SCORE_SCALE)
        dquery_t = jnp.concatenate(dquery, axis=1)
        out_ref[head * 64 : head * 64 + 64, :] = turn_back(dquery_t).astype(BF16)
        out_ref[128 + head * 64 : 128 + head * 64 + 64, :] = turn_back(dkey[...].T).astype(BF16)
        out_ref[256 + head * 64 : 256 + head * 64 + 64, :] = dvalue[...].T.astype(BF16)


def attend(qkv_t, bias, cos, sin):
    return pl.pallas_call(
        attend_kernel,
        out_shape=(
            jax.ShapeDtypeStruct((384, SEQ), BF16),
            jax.ShapeDtypeStruct((SEQ, 128), BF16),
            jax.ShapeDtypeStruct((8, SEQ), F32),
        ),
        compiler_params=pltpu.CompilerParams(vmem_limit_bytes=32 * 1024 * 1024),
        cost_estimate=pl.CostEstimate(flops=400_000_000, bytes_accessed=4_000_000, transcendentals=1_400_000),
        name="attend_forward",
    )(qkv_t, bias, cos, sin)


def attend_back(qkv_t, grad, lse, cos, sin):
    return pl.pallas_call(
        attend_back_kernel,
        out_shape=jax.ShapeDtypeStruct((384, SEQ), BF16),
        scratch_shapes=[pltpu.VMEM((SEQ, 64), F32), pltpu.VMEM((SEQ, 64), F32)],
        compiler_params=pltpu.CompilerParams(vmem_limit_bytes=48 * 1024 * 1024),
        cost_estimate=pl.CostEstimate(flops=1_000_000_000, bytes_accessed=4_000_000, transcendentals=1_400_000),
        name="attend_backward",
    )(qkv_t, grad, lse, cos, sin)


def shards(
    block_input,
    attn_gain,
    attn_bias,
    query_key_value_weight,
    query_key_value_bias,
    output_projection_weight,
    mlp_gain,
    mlp_bias,
    gate_up_projection_weight,
    down_projection_weight,
    out_grad,
):
    c = lax.axis_index("c")
    z = lax.axis_index("z")
    xh = lax.axis_index("xh")
    s = z * 2 + xh
    x_own = block_input[0]
    dy_own = out_grad[0]
    cos_np, sin_np = rotary_tables()
    cos, sin = jnp.asarray(cos_np), jnp.asarray(sin_np)

    vector = jnp.concatenate(
        [attn_gain, attn_bias, mlp_gain, mlp_bias, query_key_value_bias, jnp.zeros((128,), BF16)]
    )
    packet = jnp.concatenate([x_own, vector[None], jnp.zeros((15, D), BF16)], axis=0)
    packets = spread(packet, SHARD, 8)
    qkv_cols = query_key_value_weight.reshape(128, 3, 8, 128).transpose(2, 0, 1, 3).reshape(8, 128, 384)
    qkv_w = exchange(qkv_cols, SHARD).reshape(D, 384)
    out_w = lax.all_gather(output_projection_weight, SHARD, axis=0, tiled=True)
    gu = gate_up_projection_weight.reshape(128, 2, 4, 704).transpose(2, 0, 1, 3).reshape(4, 128, 1408)
    gu_blocks = jnp.broadcast_to(gu[:, None], (4, 2, 128, 1408)).reshape(8, 128, 1408)
    gu_w = exchange(gu_blocks, SHARD).reshape(D, 1408)
    dy_p = spread(dy_own, "z", 4).reshape(512, D)
    down_other = swap(down_projection_weight, "xh")
    first_rows = xh == 0
    down_w = jnp.concatenate(
        [
            jnp.where(first_rows, down_projection_weight, down_other),
            jnp.where(first_rows, down_other, down_projection_weight),
        ],
        axis=0,
    )

    x_blocks = packets[:, :128]
    vectors = packets[:, 128]
    gain_one = vectors[:, 0:128].reshape(1, D).astype(F32)
    bias_one = vectors[:, 128:256].reshape(1, D).astype(F32)
    gain_two = vectors[:, 256:384].reshape(1, D).astype(F32)
    bias_two = vectors[:, 384:512].reshape(1, D).astype(F32)
    qkv_bias = vectors[:, 512:896].reshape(3, 8, 128)
    qkv_bias = lax.dynamic_index_in_dim(qkv_bias, s, 1, keepdims=False).reshape(384, 1).astype(F32)

    normed_all, _ = normalize(x_blocks.reshape(SEQ, D).astype(F32))
    first_in = (normed_all * gain_one + bias_one).astype(BF16)
    qkv_t = dot(qkv_w, first_in, ((0,), (1,)))
    qkv_t, attended, lse = attend(qkv_t, qkv_bias, cos, sin)

    by_parity = attended.reshape(4, 2, 128, 128).transpose(1, 0, 2, 3).reshape(1, 2, 512, 128)
    att_blocks = jnp.broadcast_to(by_parity, (4, 2, 512, 128)).reshape(8, 512, 128)
    att_p = exchange(att_blocks, SHARD).transpose(1, 0, 2).reshape(512, D)
    x_p = lax.dynamic_index_in_dim(x_blocks.reshape(4, 2, 128, D), xh, 1, keepdims=False)
    x_p = x_p.reshape(512, D).astype(F32)
    mixed = x_p + dot(att_p, out_w, ((1,), (0,)))
    normed_two, _ = normalize(mixed)
    second_in = (normed_two * gain_two + bias_two).astype(BF16)

    gate_up = dot(second_in, gu_w, ((1,), (0,)))
    gate = gate_up[:, :704]
    up_part = gate_up[:, 704:]
    sig = jax.nn.sigmoid(gate)
    silu = gate * sig
    hidden = (silu * up_part).astype(BF16)
    dhidden = dot(dy_p, down_w, ((1,), (1,)))
    dgate = dhidden * up_part * sig * (1.0 + gate * (1.0 - sig))
    dup = dhidden * silu
    dgate_up = jnp.concatenate([dgate, dup], axis=-1).astype(BF16)
    dsecond_part = dot(dgate_up, gu_w, ((1,), (1,)))
    dsecond_blocks = exchange(dsecond_part.astype(BF16).reshape(4, 128, D), "z")
    gain_two_part = jnp.sum(dsecond_part * normed_two, axis=0)
    bias_two_part = jnp.sum(dsecond_part, axis=0)
    out_part = dot(hidden, down_w, ((1,), (0,)))
    out_blocks = exchange(out_part.astype(BF16).reshape(4, 128, D), "z")

    mixed_own = lax.dynamic_slice_in_dim(mixed, z * 128, 128, 0)
    block_output = (mixed_own + jnp.sum(out_blocks.astype(F32), axis=0)).astype(BF16)[None]
    normed_own, inverse_own = normalize(mixed_own)
    dsecond = jnp.sum(dsecond_blocks.astype(F32), axis=0)
    dmixed = dy_own.astype(F32) + norm_back(dsecond * gain_two, normed_own, inverse_own)
    dproj = dmixed.astype(BF16)
    dattended = dot(dproj, out_w, ((1,), (1,))).astype(BF16)
    dattended = exchange(dattended.reshape(128, 8, 128).transpose(1, 0, 2), SHARD).reshape(SEQ, 128)
    dproj_p = spread(dproj, "z", 4).reshape(512, D)

    gate_up_grad = dot(second_in, dgate_up, ((0,), (0,))).astype(BF16).reshape(4, 2, 128, 1408)
    down_grad = dot(hidden, dy_p, ((0,), (0,))).astype(BF16).reshape(2, 352, D)
    att_own = lax.dynamic_slice_in_dim(att_p, z * 256, 256, 1)
    out_w_grad = dot(att_own, dproj_p, ((0,), (0,))).astype(BF16).reshape(2, 128, D)
    other = 1 - c
    down_out = jnp.concatenate([down_grad, out_w_grad], axis=1)
    gu_keep = lax.dynamic_index_in_dim(gate_up_grad, c, 1, keepdims=False)
    gu_send = lax.dynamic_index_in_dim(gate_up_grad, other, 1, keepdims=False)
    do_keep = lax.dynamic_index_in_dim(down_out, c, 0, keepdims=False)
    do_send = lax.dynamic_index_in_dim(down_out, other, 0, keepdims=False)
    gu_sum = (gu_keep.astype(F32) + swap(gu_send, "c").astype(F32)).astype(BF16)
    do_sum = (do_keep.astype(F32) + swap(do_send, "c").astype(F32)).astype(BF16)
    gu_chunks = gu_sum.reshape(16, 32, 11, 128).transpose(0, 2, 1, 3).reshape(16, 352, 128)
    do_chunks = do_sum.reshape(2, 240, 8, 128).transpose(0, 2, 1, 3).reshape(16, 240, 128)
    mlp_chunks = jnp.concatenate([gu_chunks, do_chunks], axis=1)
    mlp_sum = jnp.sum(exchange(mlp_chunks, ("xh", "xl", "y")).astype(F32), axis=0).astype(BF16)
    gu_piece = move(mlp_sum[:352], lambda xl, y, c, z, xh: (z // 2, y, z % 2, 2 * xh + xl, c))
    do_piece = move(mlp_sum[352:], lambda xl, y, c, z, xh: (xl, y, xh, z, c))
    mlp_piece = jnp.concatenate([gu_piece, do_piece], axis=0)
    mlp_mine = spread(mlp_piece, ("xl", "y"), 8)
    mlp_other = swap(mlp_mine, "c")
    is_zero = c == 0
    mlp_all = jnp.stack(
        [jnp.where(is_zero, mlp_mine, mlp_other), jnp.where(is_zero, mlp_other, mlp_mine)], axis=1
    ).reshape(2, 4, 2, 592, 128)
    gu_all = mlp_all[:, :, :, :352].reshape(2, 4, 2, 11, 32, 128)
    gu_all = gu_all.transpose(1, 4, 0, 2, 3, 5).reshape(128, 4, 2, 704).transpose(0, 2, 1, 3)
    gate_up_grad_out = gu_all.reshape(128, 2 * FF).astype(F32)
    do_all = mlp_all[:, :, :, 352:].reshape(8, 2, 240, 128).transpose(1, 2, 0, 3).reshape(480, D)
    down_grad_out = do_all[:352].astype(F32)
    out_w_grad_out = do_all[352:].astype(F32)

    dqkv_t = attend_back(qkv_t, dattended, lse, cos, sin)
    dfirst_part = dot(dqkv_t, qkv_w, ((0,), (1,)))
    dfirst_blocks = exchange(dfirst_part.astype(BF16).reshape(8, 128, D), SHARD)
    dfirst = jnp.sum(dfirst_blocks.astype(F32), axis=0)
    gain_one_part = jnp.sum(dfirst_part * normed_all, axis=0)
    bias_one_part = jnp.sum(dfirst_part, axis=0)
    normed_one, inverse_one = normalize(x_own.astype(F32))
    dinput = dmixed + norm_back(dfirst * gain_one, normed_one, inverse_one)
    input_grad = dinput.astype(BF16)[None]

    qkv_grad = dot(first_in, dqkv_t, ((0,), (1,))).astype(BF16)
    qkv_chunks = qkv_grad.reshape(16, 64, 3, 128).transpose(0, 2, 1, 3).reshape(16, 192, 128)
    qkv_bias_part = jnp.sum(dqkv_t.astype(F32), axis=1).reshape(3, 128)
    small = jnp.stack([gain_one_part, bias_one_part, gain_two_part, bias_two_part]).reshape(4, 8, 128)
    small = jnp.concatenate(
        [
            small.transpose(1, 0, 2),
            jnp.broadcast_to(qkv_bias_part[None], (8, 3, 128)),
            jnp.zeros((8, 9, 128), F32),
        ],
        axis=1,
    ).astype(BF16)
    small = jnp.broadcast_to(small[:, None], (8, 2, 16, 128)).reshape(16, 16, 128)
    qkv_chunks = jnp.concatenate([qkv_chunks, small], axis=1)
    qkv_sum = jnp.sum(exchange(qkv_chunks, ("xl", "y", "c")).astype(F32), axis=0).astype(BF16)
    qkv_piece = move(qkv_sum, lambda xl, y, c, z, xh: (z // 2, (z % 2) * 2 + xh, c, 2 * xl + y // 2, y % 2))
    qkv_mine = spread(qkv_piece, ("xl", "y"), 8)
    qkv_other = swap(qkv_mine, "c")
    qkv_all = jnp.stack(
        [jnp.where(is_zero, qkv_mine, qkv_other), jnp.where(is_zero, qkv_other, qkv_mine)], axis=0
    )
    qkv_rows = qkv_all[:, :, :192].reshape(2, 8, 3, 64, 128).transpose(0, 3, 2, 1, 4)
    qkv_grad_out = qkv_rows.reshape(128, 3 * D).astype(F32)
    vectors_all = qkv_all[0, :, 192:].astype(F32)
    vector_sums = jnp.sum(vectors_all, axis=0)
    bias_all = vectors_all[:, 4:7].transpose(1, 0, 2).reshape(8, 384)
    qkv_bias_out = lax.dynamic_index_in_dim(bias_all, s, 0, keepdims=False)
    return (
        block_output,
        input_grad,
        vector_sums[0],
        vector_sums[1],
        qkv_grad_out,
        qkv_bias_out,
        out_w_grad_out,
        vector_sums[2],
        vector_sums[3],
        gate_up_grad_out,
        down_grad_out,
    )


def solution(mesh):
    fine = jax.sharding.Mesh(mesh.devices.reshape(2, 4, 2, 4, 2), ("xl", "y", "c", "z", "xh"))
    tokens = P(("xl", "y", "c"), SHARD, None)
    rows = P(SHARD, None)
    flat = P(SHARD)
    return jax.shard_map(
        shards,
        mesh=fine,
        in_specs=(tokens, flat, flat, rows, flat, rows, flat, flat, rows, rows, tokens),
        out_specs=(tokens, tokens, flat, flat, rows, flat, rows, flat, flat, rows, rows),
        check_vma=False,
    )
```

```python
import jax
import jax.numpy as jnp
import numpy as np
from jax import lax
from jax.experimental import pallas as pl
from jax.experimental.pallas import tpu as pltpu
from jax.sharding import PartitionSpec as P

D = 1024
HEADS = 16
HEAD_DIM = 64
FF = 2816
ROTARY = 16
SEQ = 1024
BLOCK = 256
UNITS = 352
PAD = 384

EPSILON = 1e-05
SCORE_SCALE = 0.125

SHARD = ("z", "xh")
PLANE = ("xl", "y")
F32 = jnp.float32
BF16 = jnp.bfloat16
MIB = 1024 * 1024

VEC_AT, QKV_AT = 1024, 1040


def normalize(values):
    center = values - jnp.mean(values, axis=-1, keepdims=True)
    variance = jnp.mean(center * center, axis=-1, keepdims=True)
    inverse = lax.rsqrt(variance + EPSILON)
    return (center * inverse, inverse)


def norm_back(scaled_grad, normed, inverse):
    return inverse * (
        scaled_grad
        - jnp.mean(scaled_grad, axis=-1, keepdims=True)
        - normed * jnp.mean(scaled_grad * normed, axis=-1, keepdims=True)
    )


def rotary_tables():
    half = ROTARY // 2
    frequency = np.float32(10000.0) ** (-np.arange(half, dtype=np.float32) * np.float32(2.0) / np.float32(ROTARY))
    angles = np.arange(SEQ, dtype=np.float32)[None, :] * frequency.astype(np.float32)[:, None]
    return np.cos(angles).astype(np.float32), np.sin(angles).astype(np.float32)


def exchange(value, axes):
    return lax.all_to_all(value, axes, 0, 0, tiled=True)


def spread(value, axes, count):
    return exchange(jnp.broadcast_to(value[None], (count,) + value.shape), axes)


def swap(value, axis):
    return lax.ppermute(value, axis, [(0, 1), (1, 0)])


def turn(value, axis, step):
    return lax.ppermute(value, axis, [(i, (i + step) % 4) for i in range(4)])


def index_of(xl, y, c, z, xh):
    return (((xl * 4 + y) * 2 + c) * 4 + z) * 2 + xh


def move(value, target):
    pairs = []
    for xl in range(2):
        for y in range(4):
            for c in range(2):
                for z in range(4):
                    for xh in range(2):
                        pairs.append((index_of(xl, y, c, z, xh), index_of(*target(xl, y, c, z, xh))))
    return lax.ppermute(value, ("xl", "y", "c", "z", "xh"), pairs)


def tie(*values):
    return lax.optimization_barrier(values)


def dot(a, b, dims=((1,), (0,))):
    return lax.dot_general(a, b, (dims, ((), ())), preferred_element_type=F32)


NT = ((1,), (1,))

ID_Y, ID_C, ID_Z, ID_XH, ID_XL = range(5)


def call(kernel, name, out_shape, args, scratch=(), flops=0, memory=16):
    first = pl.BlockSpec(memory_space=pltpu.SMEM)
    rest = [pl.BlockSpec(memory_space=pltpu.VMEM)] * (len(args) - 1)
    moved = sum(int(np.prod(a.shape)) * a.dtype.itemsize for a in list(args) + list(out_shape))
    return pl.pallas_call(
        kernel,
        out_shape=out_shape,
        in_specs=[first] + rest,
        out_specs=tuple(pl.BlockSpec(memory_space=pltpu.VMEM) for _ in out_shape),
        scratch_shapes=list(scratch),
        compiler_params=pltpu.CompilerParams(vmem_limit_bytes=memory * MIB),
        cost_estimate=pl.CostEstimate(flops=flops, bytes_accessed=moved, transcendentals=0),
        name=name,
    )(*args)


def shape(*dims, dtype=BF16):
    return jax.ShapeDtypeStruct(dims, dtype)


def turned(value, cos, sin, sign):
    a = value[0:8]
    b = value[8:16]
    return jnp.concatenate([a * cos - sign * (b * sin), b * cos + sign * (a * sin), value[16:]], axis=0)


def attend_kernel(ids, packet, other, cos_ref, sin_ref, qkv_out, attended, lse_out, w_out, xhat_out, w_rows):
    c = ids[ID_C]
    s = ids[ID_Z] * 2 + ids[ID_XH]
    mine = pl.multiple_of(c * 64, 64)
    theirs = pl.multiple_of((1 - c) * 64, 64)
    for src in range(8):
        for kind in range(3):
            lanes = slice(kind * 128, kind * 128 + 128)
            at = QKV_AT + kind * 64
            w_rows[pl.ds(src * 128 + mine, 64), lanes] = packet[src, at : at + 64, :]
            w_rows[pl.ds(src * 128 + theirs, 64), lanes] = other[src, kind * 64 : kind * 64 + 64, :]
    for kind in range(3):
        for src in range(8):
            w_out[kind * 128 : kind * 128 + 128, src * 128 : src * 128 + 128] = w_rows[
                src * 128 : src * 128 + 128, kind * 128 : kind * 128 + 128
            ].T
    vec = [packet[src, VEC_AT : VEC_AT + 16, :].astype(F32) for src in range(8)]
    gain = jnp.concatenate([v[0:1] for v in vec], axis=1)
    bias = jnp.concatenate([v[1:2] for v in vec], axis=1)
    row = lax.broadcasted_iota(jnp.int32, (16, 128), 0)
    qkv_bias = []
    for kind in range(3):
        total = jnp.zeros((16, 128), F32)
        for src in range(8):
            total += jnp.where((row >= 4) & (row < 7) & (row - 4 + 3 * src == 8 * kind + s), vec[src], 0.0)
        line = jnp.sum(total, axis=0, keepdims=True)
        qkv_bias.append(jnp.broadcast_to(line, (128, 128)).T)
    qkv_bias = jnp.concatenate(qkv_bias, axis=0)
    qkv_bias = jnp.concatenate([qkv_bias, qkv_bias], axis=1)
    for block in range(SEQ // BLOCK):
        lo = block * BLOCK
        x = jnp.concatenate(
            [
                jnp.concatenate(
                    [packet[2 * block + i, cb * 128 : cb * 128 + 128, :].astype(F32) for cb in range(8)], axis=1
                )
                for i in range(2)
            ],
            axis=0,
        )
        normed, _ = normalize(x)
        xhat_out[lo : lo + BLOCK, :] = normed.astype(BF16)
        first_in = (normed * gain + bias).astype(BF16)
        part = dot(w_out[...], first_in, NT) + qkv_bias
        cos = cos_ref[:, lo : lo + BLOCK]
        sin = sin_ref[:, lo : lo + BLOCK]
        for kind in range(3):
            for head in range(2):
                base = kind * 128 + head * 64
                full = part[base : base + 64]
                if kind < 2:
                    full = turned(full, cos, sin, 1.0)
                qkv_out[base : base + 64, lo : lo + BLOCK] = full.astype(BF16)
    row = lax.broadcasted_iota(jnp.int32, (BLOCK, BLOCK), 0)
    col = lax.broadcasted_iota(jnp.int32, (BLOCK, BLOCK), 1)
    lse_out[...] = jnp.zeros_like(lse_out)
    for block in range(SEQ // BLOCK):
        lo = block * BLOCK
        hi = lo + BLOCK
        both = []
        for head in range(2):
            keys = qkv_out[128 + head * 64 : 128 + head * 64 + 64, :hi].T
            value_t = qkv_out[256 + head * 64 : 256 + head * 64 + 64, :hi]
            query_t = qkv_out[head * 64 : head * 64 + 64, lo:hi] * jnp.bfloat16(SCORE_SCALE)
            parts = []
            if block:
                parts.append(dot(keys[:lo], query_t))
            parts.append(jnp.where(row <= col, dot(keys[lo:hi], query_t), -jnp.inf))
            scores = jnp.concatenate(parts, axis=0) if block else parts[0]
            top = jnp.max(scores, axis=0, keepdims=True)
            exps = jnp.exp(scores - top)
            total = jnp.sum(exps, axis=0, keepdims=True)
            both.append(dot(value_t, exps.astype(BF16)) / total)
            lse_out[head : head + 1, lo:hi] = top + jnp.log(total)
        out = jnp.concatenate(both, axis=0).T.astype(BF16)
        for parity in range(2):
            for zt in range(4):
                attended[2 * zt + parity, block * 128 : block * 128 + 128, :] = out[parity * 128 : parity * 128 + 128]


def weights_kernel(ids, *refs):
    pieces, (gate_w, up_w, out_w) = refs[:10], refs[10:]
    y, c = ids[ID_Y], ids[ID_C]
    gate_w[...] = jnp.zeros_like(gate_w)
    up_w[...] = jnp.zeros_like(up_w)
    for core in range(2):
        half = c if core == 0 else 1 - c
        own, before, after, far_low, far_high = pieces[core * 5 : core * 5 + 5]
        for k in range(4):
            at = pl.multiple_of(lax.rem(y - k + 4, 4) * 32, 32)
            for src in range(8):
                ref, i = ((own, src), (before, src), (far_low, src) if src < 4 else (far_high, src - 4), (after, src))[k]
                rows = pl.ds(src * 128 + at, 32)
                for cb in range(3):
                    lanes = slice(core * PAD + cb * 128, core * PAD + cb * 128 + 128)
                    gate_w[rows, lanes] = ref[i, cb * 32 : cb * 32 + 32, :]
                    up_w[rows, lanes] = ref[i, 96 + cb * 32 : 96 + cb * 32 + 32, :]
                for cb in range(4):
                    lanes = pl.ds(pl.multiple_of(half * 512 + cb * 128, 128), 128)
                    out_w[rows, lanes] = ref[i, 192 + cb * 32 : 192 + cb * 32 + 32, :]


def mlp_kernel(ids, att, x_ref, dy_ref, gain_ref, bias_ref, out_w, gate_w, up_w, down_w, *outs):
    mixed_out, second_out, hidden_out, dgate_out, dup_out, att_out, small, ds = outs
    gain = gain_ref[...]
    bias = bias_ref[...]
    gain_sum = jnp.zeros((1, D), F32)
    bias_sum = jnp.zeros((1, D), F32)
    for pair in range(2):
        rows = slice(pair * 256, pair * 256 + 256)
        a_parts = []
        x_parts = []
        for k in (2 * pair, 2 * pair + 1):
            at = slice(k * 128, k * 128 + 128)
            a_parts.append(jnp.concatenate([att[src, at, :] for src in range(8)], axis=1))
            x_parts.append(
                jnp.concatenate([x_ref[k, cb * 128 : cb * 128 + 128, :] for cb in range(8)], axis=1)
            )
        attended = jnp.concatenate(a_parts, axis=0)
        att_out[rows, :] = attended
        mixed = jnp.concatenate(x_parts, axis=0).astype(F32) + dot(attended, out_w[...])
        mixed_out[rows, :] = mixed
        normed, _ = normalize(mixed)
        second_in = (normed * gain + bias).astype(BF16)
        second_out[rows, :] = second_in
        gate = dot(second_in, gate_w[...])
        up_part = dot(second_in, up_w[...])
        sig = jax.nn.sigmoid(gate)
        silu = gate * sig
        hidden_out[rows, :] = (silu * up_part).astype(BF16)
        dhidden = dot(dy_ref[rows, :], down_w[...], NT)
        dgate = (dhidden * up_part * sig * (1.0 + gate * (1.0 - sig))).astype(BF16)
        dup = (dhidden * silu).astype(BF16)
        dgate_out[rows, :] = dgate
        dup_out[rows, :] = dup
        dsecond = dot(dgate, gate_w[...], NT) + dot(dup, up_w[...], NT)
        gain_sum += jnp.sum(dsecond * normed, axis=0, keepdims=True)
        bias_sum += jnp.sum(dsecond, axis=0, keepdims=True)
        ds[rows, :] = dsecond.astype(BF16)
    small[...] = jnp.concatenate([gain_sum, bias_sum, jnp.zeros((6, D), F32)], axis=0)


def weight_grad_kernel(ids, second_in, hidden, dgate, dup, dy, keep, send):
    y, xh, xl = ids[ID_Y], ids[ID_XH], ids[ID_XL]

    def place(j):
        to_xh, to_xl, to_y = j // 8, (j // 4) % 2, j % 4
        across = 2 * jnp.abs(xh - to_xh) + jnp.abs(xl - to_xl)
        return lax.rem(y - to_y + 4, 4) * 4 + across

    for block in range(4):
        turned_in = second_in[:, block * 256 : block * 256 + 256].T
        for which, grad in ((0, dgate), (1, dup)):
            part = dot(turned_in, grad[...]).astype(BF16)
            for target, base in ((keep, 0), (send, PAD)):
                for j in range(4):
                    for cb in range(3):
                        at = (which * 3 + cb) * 64
                        target[place(block * 4 + j), at : at + 64, :] = part[
                            j * 64 : j * 64 + 64, base + cb * 128 : base + cb * 128 + 128
                        ]
    hidden_t = hidden[...].T
    for target, base in ((keep, 0), (send, PAD)):
        part = dot(hidden_t[base : base + UNITS], dy[...]).astype(BF16)
        for h in range(2):
            for cb in range(8):
                target[place(h * 8 + cb), 384:560, :] = part[h * 176 : h * 176 + 176, cb * 128 : cb * 128 + 128]


def norm_kernel(ids, ds, dy, mixed_ref, gain_ref, out_w, dmixed_out, datt, dproj_out):
    dsecond = ds[0].astype(F32) + ds[1].astype(F32) + ds[2].astype(F32) + ds[3].astype(F32)
    own = pl.ds(pl.multiple_of(ids[ID_Z] * 128, 128), 128)
    normed, inverse = normalize(mixed_ref[own, :])
    dmixed = dy[...].astype(F32) + norm_back(dsecond * gain_ref[...], normed, inverse)
    dmixed_out[...] = dmixed
    dproj = dmixed.astype(BF16)
    dattended = dot(dproj, out_w[...], NT).astype(BF16)
    for dest in range(8):
        datt[dest] = dattended[:, dest * 128 : dest * 128 + 128]
    for dest in range(4):
        dproj_out[dest] = dproj[:, dest * 256 : dest * 256 + 256]


def attend_back_kernel(
    ids, qkv, lse_ref, datt, cos_ref, sin_ref, xhat, w_t, gain_ref, bias_ref, small, keep, send, dq_keep, dq_send,
    dkey, dvalue, dq_t, dq_rows, grad_rows
):
    c, z, xh = ids[ID_C], ids[ID_Z], ids[ID_XH]
    cos = cos_ref[...]
    sin = sin_ref[...]
    row = lax.broadcasted_iota(jnp.int32, (BLOCK, BLOCK), 0)
    col = lax.broadcasted_iota(jnp.int32, (BLOCK, BLOCK), 1)
    for head in range(2):
        dkey[...] = jnp.zeros_like(dkey)
        dvalue[...] = jnp.zeros_like(dvalue)
        key_t = qkv[128 + head * 64 : 128 + head * 64 + 64, :]
        keys = key_t.T
        values = qkv[256 + head * 64 : 256 + head * 64 + 64, :].T
        dquery = []
        for block in range(SEQ // BLOCK):
            lo = block * BLOCK
            hi = lo + BLOCK
            query_t = qkv[head * 64 : head * 64 + 64, lo:hi] * jnp.bfloat16(SCORE_SCALE)
            query = query_t.T
            grad = datt[lo:hi, head * 64 : head * 64 + 64]
            grad_t = grad.T
            lse = lse_ref[head : head + 1, lo:hi]
            parts = []
            if block:
                parts.append(jnp.exp(dot(keys[:lo], query_t) - lse))
            parts.append(jnp.where(row <= col, jnp.exp(dot(keys[lo:hi], query_t) - lse), 0.0))
            shares = jnp.concatenate(parts, axis=0) if block else parts[0]
            dshares = dot(values[:hi], grad_t)
            row_dot = jnp.sum(shares * dshares, axis=0, keepdims=True)
            dscores = (shares * (dshares - row_dot)).astype(BF16)
            dvalue[:hi] += dot(shares.astype(BF16), grad)
            dkey[:hi] += dot(dscores, query)
            dquery.append(dot(key_t[:, :hi], dscores) * SCORE_SCALE)
        dquery_t = jnp.concatenate(dquery, axis=1)
        dq_t[head * 64 : head * 64 + 64, :] = turned(dquery_t, cos, sin, -1.0).astype(BF16)
        dq_t[128 + head * 64 : 128 + head * 64 + 64, :] = turned(dkey[...].T, cos, sin, -1.0).astype(BF16)
        dq_t[256 + head * 64 : 256 + head * 64 + 64, :] = dvalue[...].T.astype(BF16)
    whole = dq_t[...]
    sums = jnp.sum(whole.astype(F32), axis=1, keepdims=True)
    product = dot(whole, xhat[...])
    weights = w_t[...].astype(F32)
    gain_part = jnp.sum(product * weights, axis=0, keepdims=True)
    bias_part = jnp.sum(sums * weights, axis=0, keepdims=True)
    grad_rows[...] = (product * gain_ref[...] + sums * bias_ref[...]).T.astype(BF16)
    lines = [
        jnp.broadcast_to(sums[kind * 128 : kind * 128 + 128], (128, 128)).T[0:1] for kind in range(3)
    ]
    for dest in range(8):
        lanes = slice(dest * 128, dest * 128 + 128)
        tile = jnp.concatenate(
            [gain_part[:, lanes], bias_part[:, lanes], small[0:2, lanes]] + lines + [jnp.zeros((9, 128), F32)], axis=0
        ).astype(BF16)
        for target, half in ((keep, c), (send, 1 - c)):
            rows = pl.ds(pl.multiple_of(dest * 128 + half * 64, 64), 64)
            for kind in range(3):
                target[dest, kind * 64 : kind * 64 + 64, :] = grad_rows[rows, kind * 128 : kind * 128 + 128]
            target[dest, 192:208, :] = tile
    dq_rows[...] = whole.T
    for k in range(4):
        base = lax.rem(z - k + 4, 4) * 256
        dq_keep[k * 128 : k * 128 + 128, :] = dq_rows[pl.ds(pl.multiple_of(base + xh * 128, 128), 128), :]
        dq_send[k * 128 : k * 128 + 128, :] = dq_rows[pl.ds(pl.multiple_of(base + (1 - xh) * 128, 128), 128), :]


def out_grad_kernel(ids, att, dproj, keep, send, held):
    c = ids[ID_C]
    for block in range(4):
        held[block * 256 : block * 256 + 256, :] = dot(
            att[:, block * 256 : block * 256 + 256].T, dproj[...]
        ).astype(BF16)
    for target, half in ((keep, c), (send, 1 - c)):
        for dest in range(8):
            rows = pl.ds(pl.multiple_of(dest * 128 + half * 64, 64), 64)
            for cb in range(2):
                target[dest, cb * 64 : cb * 64 + 64, :] = held[rows, cb * 128 : cb * 128 + 128]


def mlp_grad_kernel(ids, mine, other, gate_up, down):
    c, y, xl = ids[ID_C], ids[ID_Y], ids[ID_XL]

    def place(j):
        return jnp.abs(xl - j // 4) * 4 + lax.rem(y - j % 4 + 4, 4)

    zero = c == 0

    def wide(ref, j, which):
        return jnp.concatenate(
            [ref[j, (which * 3 + cb) * 64 : (which * 3 + cb) * 64 + 64, :].astype(F32) for cb in range(3)], axis=1
        )[:, :UNITS]

    for half in range(2):
        for which in range(2):
            parts = []
            for z in range(4):
                j = place((z // 2) * 4 + (z % 2) * 2 + half)
                a, b = wide(mine, j, which), wide(other, j, which)
                parts += [jnp.where(zero, a, b), jnp.where(zero, b, a)]
            gate_up[half * 64 : half * 64 + 64, which * FF : which * FF + FF] = jnp.concatenate(parts, axis=1)
    for cb in range(8):
        lanes = slice(cb * 128, cb * 128 + 128)
        down[pl.ds(pl.multiple_of(c * 176, 16), 176), lanes] = mine[place(cb), 384:560, :].astype(F32)
        down[pl.ds(pl.multiple_of((1 - c) * 176, 16), 176), lanes] = other[place(cb), 384:560, :].astype(F32)


def qkv_grad_kernel(ids, mine, other, qkv, out_w, vectors):
    c = ids[ID_C]
    s = ids[ID_Z] * 2 + ids[ID_XH]
    for ref, half in ((mine, c), (other, 1 - c)):
        rows = pl.ds(pl.multiple_of(half * 64, 64), 64)
        for src in range(8):
            for kind in range(3):
                lanes = slice(kind * D + src * 128, kind * D + src * 128 + 128)
                qkv[rows, lanes] = ref[src, kind * 64 : kind * 64 + 64, :].astype(F32)
        for z in range(4):
            for cb in range(2):
                at = 208 + cb * 64
                lanes = slice(z * 256 + cb * 128, z * 256 + cb * 128 + 128)
                out_w[rows, lanes] = (
                    ref[2 * z, at : at + 64, :].astype(F32) + ref[2 * z + 1, at : at + 64, :].astype(F32)
                )
    tiles = [mine[src, 192:208, :].astype(F32) for src in range(8)]
    total = tiles[0]
    for tile in tiles[1:]:
        total = total + tile
    row = lax.broadcasted_iota(jnp.int32, (16, 128), 0)
    lines = []
    for i in range(3):
        block = 3 * s + i
        found = jnp.zeros((16, 128), F32)
        for src in range(8):
            for kind in range(3):
                found += jnp.where((row == 4 + kind) & (block == 8 * kind + src), tiles[src], 0.0)
        lines.append(jnp.sum(found, axis=0, keepdims=True))
    vectors[...] = jnp.concatenate([total[0:4]] + lines + [jnp.zeros((1, 128), F32)], axis=0)


def shards(
    block_input,
    attn_gain,
    attn_bias,
    query_key_value_weight,
    query_key_value_bias,
    output_projection_weight,
    mlp_gain,
    mlp_bias,
    gate_up_projection_weight,
    down_projection_weight,
    out_grad,
):
    y = lax.axis_index("y")
    c = lax.axis_index("c")
    z = lax.axis_index("z")
    xh = lax.axis_index("xh")
    xl = lax.axis_index("xl")
    ids = jnp.stack([y, c, z, xh, xl]).astype(jnp.int32)
    x_own = block_input[0]
    dy_own = out_grad[0]
    cos_np, sin_np = rotary_tables()
    cos, sin = jnp.asarray(cos_np), jnp.asarray(sin_np)

    gu_rows = lax.dynamic_slice_in_dim(gate_up_projection_weight, y * 32, 32, 0).reshape(32, 2, 4, 2, UNITS)
    gu_rows = lax.dynamic_index_in_dim(gu_rows, c, 3, keepdims=False)
    gu_rows = jnp.pad(gu_rows, ((0, 0), (0, 0), (0, 0), (0, PAD - UNITS))).reshape(32, 2, 4, 3, 128)
    gu_part = jnp.broadcast_to(gu_rows.transpose(2, 1, 3, 0, 4).reshape(4, 1, 192, 128), (4, 2, 192, 128))
    out_rows = lax.dynamic_slice(output_projection_weight, (y * 32, c * 512), (32, 512))
    out_part = out_rows.reshape(32, 4, 128).transpose(1, 0, 2).reshape(128, 128)
    tail = jnp.broadcast_to(out_part[None], (8, 128, 128))
    piece = exchange(jnp.concatenate([gu_part.reshape(8, 192, 128), tail], axis=1), SHARD)

    x_part = x_own.reshape(128, 8, 128).transpose(1, 0, 2).reshape(D, 128)
    vec = jnp.concatenate(
        [
            jnp.stack([attn_gain, attn_bias, mlp_gain, mlp_bias]),
            query_key_value_bias.reshape(3, 128),
            jnp.zeros((9, 128), BF16),
        ]
    )
    qkv_rows = lax.dynamic_slice_in_dim(query_key_value_weight, c * 64, 64, 0)
    qkv_part = qkv_rows.reshape(64, 3, 8, 128).transpose(2, 1, 0, 3).reshape(8, 192, 128)
    head = jnp.broadcast_to(jnp.concatenate([x_part, vec])[None], (8, QKV_AT, 128))
    packet = jnp.concatenate([head, qkv_part], axis=1)
    piece, packet = tie(piece, packet)
    packet = exchange(packet, SHARD)

    before = turn(piece, "y", 1)
    after = turn(piece, "y", -1)
    pieces = [piece, before, after, turn(before[:4], "y", 1), turn(after[4:], "y", -1)]
    pieces += [swap(p, "c") for p in pieces]
    gate_w, up_w, out_w = call(
        weights_kernel, "weights", (shape(D, 2 * PAD), shape(D, 2 * PAD), shape(D, D)), (ids, *pieces)
    )
    packet, dy_now = tie(packet, dy_own)

    qkv_other = swap(packet[:, QKV_AT:], "c")
    qkv_t, att_blocks, lse, w_t, xhat = call(
        attend_kernel,
        "attend_forward",
        (shape(384, SEQ), shape(8, 512, 128), shape(8, SEQ, dtype=F32), shape(384, D), shape(SEQ, D)),
        (ids, packet, qkv_other, cos, sin),
        scratch=[pltpu.VMEM((D, 384), BF16)],
        flops=1_300_000_000,
    )
    att_blocks, down_now = tie(att_blocks, down_projection_weight)
    att = exchange(att_blocks, SHARD)
    down_other = swap(down_now, "xh")
    own_first = xh == c
    filler = jnp.zeros((PAD - UNITS, D), BF16)
    down_w = jnp.concatenate(
        [
            jnp.where(own_first, down_now, down_other),
            filler,
            jnp.where(own_first, down_other, down_now),
            filler,
        ],
        axis=0,
    )

    dy_before = turn(dy_now, "z", 1)
    dy_after = turn(dy_now, "z", -1)
    dy_far = jnp.concatenate([turn(dy_before[:64], "z", 1), turn(dy_after[64:], "z", -1)], axis=0)
    dy_p = jnp.zeros((512, D), BF16)
    for k, value in enumerate((dy_now, dy_before, dy_far, dy_after)):
        dy_p = lax.dynamic_update_slice_in_dim(dy_p, value, lax.rem(z - k + 4, 4) * 128, 0)
    vecs = packet[:, VEC_AT : VEC_AT + 4].astype(F32).transpose(1, 0, 2).reshape(4, 1, D)
    gain_one, bias_one, gain_two, bias_two = vecs[0], vecs[1], vecs[2], vecs[3]
    x_p = lax.dynamic_index_in_dim(packet[:, :D].reshape(4, 2, D, 128), xh, 1, keepdims=False)
    w_t_other = swap(w_t, "xh")

    mixed, second_in, hidden, dgate, dup, att_p, mlp_small, ds = call(
        mlp_kernel,
        "mlp",
        (
            shape(512, D, dtype=F32),
            shape(512, D),
            shape(512, 2 * PAD),
            shape(512, 2 * PAD),
            shape(512, 2 * PAD),
            shape(512, D),
            shape(8, D, dtype=F32),
            shape(512, D),
        ),
        (ids, att, x_p, dy_p, gain_two, bias_two, out_w, gate_w, up_w, down_w),
        flops=5_000_000_000,
        memory=24,
    )
    ds = exchange(ds.reshape(4, 128, D), "z")
    dmixed, datt, dproj = call(
        norm_kernel,
        "norm_backward",
        (shape(128, D, dtype=F32), shape(8, 128, 128), shape(4, 128, 256)),
        (ids, ds, dy_own, mixed, gain_two, out_w),
        flops=300_000_000,
    )
    datt = exchange(datt, SHARD).reshape(SEQ, 128)
    datt, dproj = tie(datt, dproj)
    dproj_p = exchange(dproj, "z").reshape(512, 256)

    keep, send = call(
        weight_grad_kernel,
        "weight_grad",
        (shape(16, 560, 128), shape(16, 560, 128)),
        (ids, second_in, hidden, dgate, dup, dy_p),
        flops=2_500_000_000,
    )
    mlp_chunks = (keep.astype(F32) + swap(send, "c").astype(F32)).astype(BF16).reshape(4, 4, 560, 128)
    mlp_y = mlp_chunks[0].astype(F32)
    for k in (1, 2, 3):
        mlp_y = mlp_y + turn(mlp_chunks[k], "y", -k).astype(F32)
    mlp_y = mlp_y.astype(BF16)
    out_part = dot(hidden, down_w).astype(BF16)
    total = lax.dynamic_slice_in_dim(mixed, z * 128, 128, 0)
    total = total + lax.dynamic_slice_in_dim(out_part, z * 128, 128, 0).astype(F32)
    for k in (1, 2, 3):
        part = lax.dynamic_slice_in_dim(out_part, lax.rem(z - k + 4, 4) * 128, 128, 0)
        total = total + turn(part, "z", -k).astype(F32)
    block_output = total.astype(BF16)[None]

    qkv_keep, qkv_send, dq_keep, dq_send = call(
        attend_back_kernel,
        "attend_backward",
        (shape(8, 208, 128), shape(8, 208, 128), shape(512, 384), shape(512, 384)),
        (ids, qkv_t, lse, datt, cos, sin, xhat, w_t, gain_one, bias_one, mlp_small),
        scratch=[
            pltpu.VMEM((SEQ, HEAD_DIM), F32),
            pltpu.VMEM((SEQ, HEAD_DIM), F32),
            pltpu.VMEM((384, SEQ), BF16),
            pltpu.VMEM((SEQ, 384), BF16),
            pltpu.VMEM((D, 384), BF16),
        ],
        flops=2_000_000_000,
        memory=24,
    )

    qkv_send, mlp_y = tie(qkv_send, mlp_y)
    mlp_sum = mlp_y[0].astype(F32)
    for k in (1, 2, 3):
        mlp_sum = mlp_sum + move(
            mlp_y[k], lambda xl, y, c, z, xh, k=k: (xl ^ (k & 1), y, c, z, xh ^ (k >> 1))
        ).astype(F32)
    mlp_sum = mlp_sum.astype(BF16)
    out_keep, out_send = call(
        out_grad_kernel,
        "out_grad",
        (shape(8, 128, 128), shape(8, 128, 128)),
        (ids, att_p, dproj_p),
        scratch=[pltpu.VMEM((D, 256), BF16)],
        flops=270_000_000,
    )
    chunks = jnp.concatenate(
        [
            (qkv_keep.astype(F32) + swap(qkv_send, "c").astype(F32)).astype(BF16),
            (out_keep.astype(F32) + swap(out_send, "c").astype(F32)).astype(BF16),
        ],
        axis=1,
    )
    grad_sum = jnp.sum(exchange(chunks, PLANE).astype(F32), axis=0).astype(BF16)
    grad_sum, mlp_sum = tie(grad_sum, mlp_sum)
    grad_piece = move(
        grad_sum, lambda xl, y, c, z, xh: (z // 2, (z % 2) * 2 + xh, c, 2 * xl + y // 2, y % 2)
    )
    gu_piece = move(
        mlp_sum[:384], lambda xl, y, c, z, xh: (z // 2, (z % 2) * 2 + y % 2, c, 2 * xh + xl, y // 2)
    )
    do_piece = move(mlp_sum[384:], lambda xl, y, c, z, xh: (xl, y, xh, z, c))
    mlp_piece = jnp.concatenate([gu_piece, do_piece], axis=0)
    mlp_near = jnp.stack([mlp_piece] + [turn(mlp_piece, "y", k) for k in (1, 2, 3)])
    mlp_mine = jnp.stack([mlp_near, swap(mlp_near, "xl")]).reshape(8, 560, 128)
    mlp_other = swap(mlp_mine, "c")
    gate_up_grad, down_grad = call(
        mlp_grad_kernel,
        "mlp_grad",
        (shape(128, 2 * FF, dtype=F32), shape(UNITS, D, dtype=F32)),
        (ids, mlp_mine, mlp_other),
    )

    grad_mine = spread(grad_piece, PLANE, 8)
    grad_other = swap(grad_mine, "c")
    qkv_grad, out_w_grad, vectors = call(
        qkv_grad_kernel,
        "qkv_grad",
        (shape(128, 3 * D, dtype=F32), shape(128, D, dtype=F32), shape(8, 128, dtype=F32)),
        (ids, grad_mine, grad_other),
    )

    dfirst_part = (dot(dq_keep, w_t) + dot(swap(dq_send, "xh"), w_t_other)).astype(BF16)
    dfirst = dfirst_part[:128].astype(F32)
    for k in (1, 2, 3):
        dfirst = dfirst + turn(dfirst_part[k * 128 : k * 128 + 128], "z", -k).astype(F32)
    normed_one, inverse_one = normalize(x_own.astype(F32))
    input_grad = (dmixed + norm_back(dfirst * gain_one, normed_one, inverse_one)).astype(BF16)[None]
    return (
        block_output,
        input_grad,
        vectors[0],
        vectors[1],
        qkv_grad,
        vectors[4:7].reshape(384),
        out_w_grad,
        vectors[2],
        vectors[3],
        gate_up_grad,
        down_grad,
    )


def solution(mesh):
    fine = jax.sharding.Mesh(mesh.devices.reshape(2, 4, 2, 4, 2), ("xl", "y", "c", "z", "xh"))
    tokens = P(("xl", "y", "c"), SHARD, None)
    rows = P(SHARD, None)
    flat = P(SHARD)
    return jax.shard_map(
        shards,
        mesh=fine,
        in_specs=(tokens, flat, flat, rows, flat, rows, flat, flat, rows, rows, tokens),
        out_specs=(tokens, tokens, flat, flat, rows, flat, rows, flat, flat, rows, rows),
        check_vma=False,
    )
```

```python
import jax
import jax.numpy as jnp
import numpy as np
from jax import lax
from jax.experimental import pallas as pl
from jax.experimental.pallas import tpu as pltpu
from jax.sharding import PartitionSpec as P

D = 1024
HEADS = 16
HEAD_DIM = 64
FF = 2816
ROTARY = 16
SEQ = 1024
BLOCK = 256
UNITS = 352
PAD = 384

EPSILON = 1e-05
SCORE_SCALE = 0.125

SHARD = ("z", "xh")
PLANE = ("xl", "y")
F32 = jnp.float32
BF16 = jnp.bfloat16
MIB = 1024 * 1024

VEC_AT, QKV_AT, GU_AT = 1024, 1040, 1232


def normalize(values):
    center = values - jnp.mean(values, axis=-1, keepdims=True)
    variance = jnp.mean(center * center, axis=-1, keepdims=True)
    inverse = lax.rsqrt(variance + EPSILON)
    return (center * inverse, inverse)


def norm_back(scaled_grad, normed, inverse):
    return inverse * (
        scaled_grad
        - jnp.mean(scaled_grad, axis=-1, keepdims=True)
        - normed * jnp.mean(scaled_grad * normed, axis=-1, keepdims=True)
    )


def rotary_tables():
    half = ROTARY // 2
    frequency = np.float32(10000.0) ** (-np.arange(half, dtype=np.float32) * np.float32(2.0) / np.float32(ROTARY))
    angles = np.arange(SEQ, dtype=np.float32)[None, :] * frequency.astype(np.float32)[:, None]
    return np.cos(angles).astype(np.float32), np.sin(angles).astype(np.float32)


def exchange(value, axes):
    return lax.all_to_all(value, axes, 0, 0, tiled=True)


def spread(value, axes, count):
    return exchange(jnp.broadcast_to(value[None], (count,) + value.shape), axes)


def swap(value, axis):
    return lax.ppermute(value, axis, [(0, 1), (1, 0)])


def turn(value, axis, step):
    return lax.ppermute(value, axis, [(i, (i + step) % 4) for i in range(4)])


def index_of(xl, y, c, z, xh):
    return (((xl * 4 + y) * 2 + c) * 4 + z) * 2 + xh


def move(value, target):
    pairs = []
    for xl in range(2):
        for y in range(4):
            for c in range(2):
                for z in range(4):
                    for xh in range(2):
                        pairs.append((index_of(xl, y, c, z, xh), index_of(*target(xl, y, c, z, xh))))
    return lax.ppermute(value, ("xl", "y", "c", "z", "xh"), pairs)


def tie(*values):
    return lax.optimization_barrier(values)


def dot(a, b, dims=((1,), (0,))):
    return lax.dot_general(a, b, (dims, ((), ())), preferred_element_type=F32)


NT = ((1,), (1,))

ID_Y, ID_C, ID_Z, ID_XH, ID_XL = range(5)


class Part:
    def __init__(self, array, count, dims, views):
        self.array, self.shape, self.dtype, self.views = array, (count,) + dims, array.dtype, views


class Later:
    def __init__(self, copies, buffer):
        self.copies, self.buffer = copies, buffer

    def arrive(self):
        for copy in self.copies:
            copy.wait()
        self.copies = []
        return self.buffer

    def __getitem__(self, index):
        return self.arrive()[index]


class Result:
    def __init__(self, copy, buffer):
        self.copy, self.buffer, self.sent = copy, buffer, False

    def __setitem__(self, index, value):
        self.buffer[index] = value

    def __getitem__(self, index):
        return self.buffer[index]

    def send(self):
        if not self.sent:
            self.copy.start()
            self.sent = True


def call(kernel, name, out_shape, args, scratch=(), moved=1):
    count, outs, own = len(args) - 1, len(out_shape), len(scratch)

    def body(ids, *refs):
        sources, rest = refs[:count], refs[count:]
        targets, mine, rest = rest[:outs], rest[outs : outs + own], rest[outs + own :]
        buffers, results, (sems, out_sems) = rest[:count], rest[count:-2], rest[-2:]
        inputs = []
        at = 0
        for i in range(count):
            if isinstance(args[i + 1], Part):
                views = args[i + 1].views(sources[i], ids)
                copies = [
                    pltpu.make_async_copy(view, buffers[i].at[j], sems.at[at + j]) for j, view in enumerate(views)
                ]
            else:
                copies = [pltpu.make_async_copy(sources[i], buffers[i], sems.at[at])]
            at += len(copies)
            for copy in copies:
                copy.start()
            inputs.append(Later(copies, buffers[i]))
        outputs = [
            Result(pltpu.make_async_copy(results[i], targets[i], out_sems.at[i]), results[i]) for i in range(outs)
        ]
        kernel(ids, *inputs, *outputs, *mine)
        for value in inputs:
            value.arrive()
        for value in outputs:
            value.send()
        for value in outputs:
            value.copy.wait()

    flights = sum(a.shape[0] if isinstance(a, Part) else 1 for a in args[1:])
    return pl.pallas_call(
        body,
        out_shape=out_shape,
        in_specs=[pl.BlockSpec(memory_space=pltpu.SMEM)] + [pl.BlockSpec(memory_space=pltpu.HBM)] * count,
        out_specs=tuple(pl.BlockSpec(memory_space=pltpu.HBM) for _ in out_shape),
        scratch_shapes=list(scratch)
        + [pltpu.VMEM(a.shape, a.dtype) for a in list(args[1:]) + list(out_shape)]
        + [pltpu.SemaphoreType.DMA((flights,)), pltpu.SemaphoreType.DMA((outs,))],
        compiler_params=pltpu.CompilerParams(vmem_limit_bytes=60 * MIB),
        cost_estimate=pl.CostEstimate(flops=0, bytes_accessed=moved, transcendentals=0),
        name=name,
    )(*[a.array if isinstance(a, Part) else a for a in args])


def shape(*dims, dtype=BF16):
    return jax.ShapeDtypeStruct(dims, dtype)


def turned(value, cos, sin, sign):
    a = value[0:8]
    b = value[8:16]
    return jnp.concatenate([a * cos - sign * (b * sin), b * cos + sign * (a * sin), value[16:]], axis=0)


def qkv_weights(c, packet, other, w_rows, w_out):
    mine = pl.multiple_of(c * 64, 64)
    theirs = pl.multiple_of((1 - c) * 64, 64)
    for src in range(8):
        for kind in range(3):
            lanes = slice(kind * 128, kind * 128 + 128)
            at = QKV_AT + kind * 64
            w_rows[pl.ds(src * 128 + mine, 64), lanes] = packet[0, src, at : at + 64, :]
            w_rows[pl.ds(src * 128 + theirs, 64), lanes] = other[src, kind * 64 : kind * 64 + 64, :]
    for kind in range(3):
        for src in range(8):
            w_out[kind * 128 : kind * 128 + 128, src * 128 : src * 128 + 128] = w_rows[
                src * 128 : src * 128 + 128, kind * 128 : kind * 128 + 128
            ].T


def normed_kernel(ids, packet, xhat_out):
    for block in range(8):
        x = jnp.concatenate([packet[0, block, cb * 128 : cb * 128 + 128, :].astype(F32) for cb in range(8)], axis=1)
        xhat_out[block * 128 : block * 128 + 128, :] = normalize(x)[0].astype(BF16)


def attend_kernel(ids, packet, other, cos_ref, sin_ref, qkv_out, attended, lse_out, w_out, w_rows):
    c = ids[ID_C]
    s = ids[ID_Z] * 2 + ids[ID_XH]
    qkv_weights(c, packet, other, w_rows, w_out)
    w_out.send()
    vec = [packet[0, src, VEC_AT : VEC_AT + 16, :].astype(F32) for src in range(8)]
    gain = jnp.concatenate([v[0:1] for v in vec], axis=1)
    bias = jnp.concatenate([v[1:2] for v in vec], axis=1)
    row = lax.broadcasted_iota(jnp.int32, (16, 128), 0)
    qkv_bias = []
    for kind in range(3):
        total = jnp.zeros((16, 128), F32)
        for src in range(8):
            total += jnp.where((row >= 4) & (row < 7) & (row - 4 + 3 * src == 8 * kind + s), vec[src], 0.0)
        line = jnp.sum(total, axis=0, keepdims=True)
        qkv_bias.append(jnp.broadcast_to(line, (128, 128)).T)
    qkv_bias = jnp.concatenate(qkv_bias, axis=0)
    qkv_bias = jnp.concatenate([qkv_bias, qkv_bias], axis=1)
    for block in range(SEQ // BLOCK):
        lo = block * BLOCK
        x = jnp.concatenate(
            [
                jnp.concatenate(
                    [packet[0, 2 * block + i, cb * 128 : cb * 128 + 128, :].astype(F32) for cb in range(8)], axis=1
                )
                for i in range(2)
            ],
            axis=0,
        )
        normed, _ = normalize(x)
        first_in = (normed * gain + bias).astype(BF16)
        part = dot(w_out[...], first_in, NT) + qkv_bias
        cos = cos_ref[:, lo : lo + BLOCK]
        sin = sin_ref[:, lo : lo + BLOCK]
        for kind in range(3):
            for head in range(2):
                base = kind * 128 + head * 64
                full = part[base : base + 64]
                if kind < 2:
                    full = turned(full, cos, sin, 1.0)
                qkv_out[base : base + 64, lo : lo + BLOCK] = full.astype(BF16)
    qkv_out.send()
    row = lax.broadcasted_iota(jnp.int32, (BLOCK, BLOCK), 0)
    col = lax.broadcasted_iota(jnp.int32, (BLOCK, BLOCK), 1)
    lse_out[...] = jnp.zeros((8, SEQ), F32)
    for block in range(SEQ // BLOCK):
        lo = block * BLOCK
        hi = lo + BLOCK
        both = []
        for head in range(2):
            keys = qkv_out[128 + head * 64 : 128 + head * 64 + 64, :hi].T
            value_t = qkv_out[256 + head * 64 : 256 + head * 64 + 64, :hi]
            query_t = qkv_out[head * 64 : head * 64 + 64, lo:hi] * jnp.bfloat16(SCORE_SCALE)
            parts = []
            if block:
                parts.append(dot(keys[:lo], query_t))
            parts.append(jnp.where(row <= col, dot(keys[lo:hi], query_t), -jnp.inf))
            scores = jnp.concatenate(parts, axis=0) if block else parts[0]
            top = jnp.max(scores, axis=0, keepdims=True)
            exps = jnp.exp(scores - top)
            total = jnp.sum(exps, axis=0, keepdims=True)
            both.append(dot(value_t, exps.astype(BF16)) / total)
            lse_out[head : head + 1, lo:hi] = top + jnp.log(total)
        out = jnp.concatenate(both, axis=0).T.astype(BF16)
        for parity in range(2):
            for zt in range(4):
                attended[2 * zt + parity, block * 128 : block * 128 + 128, :] = out[parity * 128 : parity * 128 + 128]


def weights_kernel(ids, p0, p1, p2, p3, p4, p5, p6, p7, gate_w, up_w, out_w):
    y, c = ids[ID_Y], ids[ID_C]
    for k, refs in enumerate(((p0, p4), (p1, p5), (p2, p6), (p3, p7))):
        at = pl.multiple_of(lax.rem(y - k + 4, 4) * 32, 32)
        for core, ref in enumerate(refs):
            half = c if core == 0 else 1 - c
            for src in range(8):
                rows = pl.ds(src * 128 + at, 32)
                for cb in range(3):
                    lanes = slice(core * PAD + cb * 128, core * PAD + cb * 128 + 128)
                    gate_w[rows, lanes] = ref[src, cb * 32 : cb * 32 + 32, :]
                    up_w[rows, lanes] = ref[src, 96 + cb * 32 : 96 + cb * 32 + 32, :]
                for cb in range(4):
                    lanes = pl.ds(pl.multiple_of(half * 512 + cb * 128, 128), 128)
                    out_w[rows, lanes] = ref[src, 192 + cb * 32 : 192 + cb * 32 + 32, :]


def assemble_down(ids, own, other, down_w):
    swapped = jnp.where(ids[ID_XH] == ids[ID_C], 0, PAD)
    down_w[pl.ds(pl.multiple_of(swapped, 128), UNITS), :] = own[...]
    down_w[pl.ds(pl.multiple_of(PAD - swapped, 128), UNITS), :] = other[...]
    for base in (UNITS, PAD + UNITS):
        down_w[base : base + PAD - UNITS, :] = jnp.zeros((PAD - UNITS, D), BF16)


def cotangent(parts):
    return jnp.concatenate([part[...] for part in parts], axis=0)


def mlp_kernel(
    ids, out_w, att, x_ref, gate_w, up_w, gain_ref, bias_ref, dy0, dy1, dy2, dy3, down_own, down_other, mixed_own, att_out, small, ds, keep, send, out0, out1, out2, out3, down_w, second_out, hidden_out, dgate_out, dup_out, held
):
    z = ids[ID_Z]
    gain = gain_ref[...]
    bias = bias_ref[...]
    gain_sum = jnp.zeros((1, D), F32)
    bias_sum = jnp.zeros((1, D), F32)
    for pair in range(2):
        rows = slice(pair * 256, pair * 256 + 256)
        a_parts = []
        x_parts = []
        for k in (2 * pair, 2 * pair + 1):
            place = lax.rem(z - k + 4, 4)
            at = pl.ds(pl.multiple_of(place * 128, 128), 128)
            a_parts.append(jnp.concatenate([att[src, at, :] for src in range(8)], axis=1))
            x_parts.append(
                jnp.concatenate([x_ref[k, cb * 128 : cb * 128 + 128, :] for cb in range(8)], axis=1)
            )
        attended = jnp.concatenate(a_parts, axis=0)
        att_out[rows, :] = attended
        mixed = jnp.concatenate(x_parts, axis=0).astype(F32) + dot(attended, out_w[...])
        if pair == 0:
            mixed_own[...] = mixed[:128]
        normed, _ = normalize(mixed)
        second_in = (normed * gain + bias).astype(BF16)
        second_out[rows, :] = second_in
        gate = dot(second_in, gate_w[...])
        up_part = dot(second_in, up_w[...])
        sig = jax.nn.sigmoid(gate)
        silu = gate * sig
        hidden_out[rows, :] = (silu * up_part).astype(BF16)
        dy = cotangent((dy0, dy1, dy2, dy3)[2 * pair : 2 * pair + 2])
        if pair == 0:
            assemble_down(ids, down_own, down_other, down_w)
        dhidden = dot(dy, down_w[...], NT)
        dgate = (dhidden * up_part * sig * (1.0 + gate * (1.0 - sig))).astype(BF16)
        dup = (dhidden * silu).astype(BF16)
        dgate_out[rows, :] = dgate
        dup_out[rows, :] = dup
        dsecond = dot(dgate, gate_w[...], NT) + dot(dup, up_w[...], NT)
        gain_sum += jnp.sum(dsecond * normed, axis=0, keepdims=True)
        bias_sum += jnp.sum(dsecond, axis=0, keepdims=True)
        low = dsecond.astype(BF16)
        for i in range(2):
            ds[lax.rem(z - (2 * pair + i) + 4, 4)] = low[i * 128 : i * 128 + 128]
    small[...] = jnp.concatenate([gain_sum, bias_sum, jnp.zeros((6, D), F32)], axis=0)
    ds.send()
    att_out.send()

    y, c, xh, xl = ids[ID_Y], ids[ID_C], ids[ID_XH], ids[ID_XL]

    def place(to_y):
        return lax.rem(y - to_y + 4, 4)

    for block in range(4):
        turned_in = second_out[:, block * 256 : block * 256 + 256].T
        for which, grad in ((0, dgate_out), (1, dup_out)):
            part = dot(turned_in, grad[...]).astype(BF16)
            for target, base in ((keep, 0), (send, PAD)):
                for i in range(16):
                    owner, to_xl, to_y = block * 2 + i // 8, (i // 4) % 2, i % 4
                    for cb in range(3):
                        at = (owner * 2 + to_xl) * 96 + (which * 3 + cb) * 16
                        target[place(to_y), at : at + 16, :] = part[
                            i * 16 : i * 16 + 16, base + cb * 128 : base + cb * 128 + 128
                        ]
    hidden_t = hidden_out[...].T
    held[...] = dot(hidden_t, cotangent((dy0, dy1, dy2, dy3))).astype(BF16)
    for target, half in ((keep, c), (send, 1 - c)):
        for base, to_xh in ((0, c), (PAD, 1 - c)):
            for to_xl in range(2):
                rows = pl.ds(pl.multiple_of(1536 + jnp.abs(xh - to_xh) * 352 + to_xl * 176, 16), 176)
                for cb in range(4):
                    lanes = pl.ds(pl.multiple_of(half * 512 + cb * 128, 128), 128)
                    target[place(cb), rows, :] = held[base + to_xl * 176 : base + to_xl * 176 + 176, lanes]
    send.send()
    keep.send()
    for pair in range(2):
        part = dot(hidden_out[pair * 256 : pair * 256 + 256, :], down_w[...]).astype(BF16)
        ((out0, out1), (out2, out3))[pair][0][...] = part[:128]
        ((out0, out1), (out2, out3))[pair][1][...] = part[128:]


def norm_kernel(ids, ds, dy, mixed_ref, gain_ref, out_w, dmixed_out, blocks):
    dsecond = ds[0].astype(F32) + ds[1].astype(F32) + ds[2].astype(F32) + ds[3].astype(F32)
    normed, inverse = normalize(mixed_ref[...])
    dmixed = dy[...].astype(F32) + norm_back(dsecond * gain_ref[...], normed, inverse)
    dmixed_out[...] = dmixed
    dproj = dmixed.astype(BF16)
    dattended = dot(dproj, out_w[...], NT).astype(BF16)
    for dest in range(8):
        blocks[dest, :128, :] = dattended[:, dest * 128 : dest * 128 + 128]
        for cb in range(2):
            at = (dest // 2) * 256 + cb * 128
            blocks[dest, 128 + cb * 128 : 256 + cb * 128, :] = dproj[:, at : at + 128]


def attend_back_kernel(
    ids, blocks, qkv, lse_ref, cos_ref, sin_ref, xhat, w_t, gain_ref, bias_ref, small, att, keep, send, dq_keep,
    dq_send, dkey, dvalue, dq_t, dq_rows, grad_rows, out_rows
):
    c, z, xh = ids[ID_C], ids[ID_Z], ids[ID_XH]
    cos = cos_ref[...]
    sin = sin_ref[...]
    row = lax.broadcasted_iota(jnp.int32, (BLOCK, BLOCK), 0)
    col = lax.broadcasted_iota(jnp.int32, (BLOCK, BLOCK), 1)
    for head in range(2):
        dkey[...] = jnp.zeros_like(dkey)
        dvalue[...] = jnp.zeros_like(dvalue)
        key_t = qkv[128 + head * 64 : 128 + head * 64 + 64, :]
        keys = key_t.T
        values = qkv[256 + head * 64 : 256 + head * 64 + 64, :].T
        dquery = []
        for block in range(SEQ // BLOCK):
            lo = block * BLOCK
            hi = lo + BLOCK
            query_t = qkv[head * 64 : head * 64 + 64, lo:hi] * jnp.bfloat16(SCORE_SCALE)
            query = query_t.T
            grad = jnp.concatenate(
                [blocks[2 * block + i, :128, head * 64 : head * 64 + 64] for i in range(2)], axis=0
            )
            grad_t = grad.T
            lse = lse_ref[head : head + 1, lo:hi]
            parts = []
            if block:
                parts.append(jnp.exp(dot(keys[:lo], query_t) - lse))
            parts.append(jnp.where(row <= col, jnp.exp(dot(keys[lo:hi], query_t) - lse), 0.0))
            shares = jnp.concatenate(parts, axis=0) if block else parts[0]
            dshares = dot(values[:hi], grad_t)
            row_dot = jnp.sum(shares * dshares, axis=0, keepdims=True)
            dscores = (shares * (dshares - row_dot)).astype(BF16)
            dvalue[:hi] += dot(shares.astype(BF16), grad)
            dkey[:hi] += dot(dscores, query)
            dquery.append(dot(key_t[:, :hi], dscores) * SCORE_SCALE)
        dquery_t = jnp.concatenate(dquery, axis=1)
        dq_t[head * 64 : head * 64 + 64, :] = turned(dquery_t, cos, sin, -1.0).astype(BF16)
        dq_t[128 + head * 64 : 128 + head * 64 + 64, :] = turned(dkey[...].T, cos, sin, -1.0).astype(BF16)
        dq_t[256 + head * 64 : 256 + head * 64 + 64, :] = dvalue[...].T.astype(BF16)
    whole = dq_t[...]
    sums = jnp.sum(whole.astype(F32), axis=1, keepdims=True)
    product = dot(whole, xhat[...])
    weights = w_t[...].astype(F32)
    gain_part = jnp.sum(product * weights, axis=0, keepdims=True)
    bias_part = jnp.sum(sums * weights, axis=0, keepdims=True)
    grad_rows[...] = (product * gain_ref[...] + sums * bias_ref[...]).T
    dproj = jnp.concatenate(
        [
            jnp.concatenate(
                [blocks[2 * lax.rem(z - k + 4, 4) + xh, 128 + cb * 128 : 256 + cb * 128, :] for cb in range(2)], axis=1
            )
            for k in range(4)
        ],
        axis=0,
    )
    for block in range(4):
        rows = slice(block * 256, block * 256 + 256)
        out_rows[rows, :] = dot(att[:, rows].T, dproj)
    lines = [
        jnp.broadcast_to(sums[kind * 128 : kind * 128 + 128], (128, 128)).T[0:1] for kind in range(3)
    ]
    filler = jnp.zeros((7, 128), F32)
    for dest in range(8):
        lanes = slice(dest * 128, dest * 128 + 128)
        lines_here = [gain_part[:, lanes], bias_part[:, lanes], small[0:1, lanes], small[1:2, lanes]] + lines
        lines_here.append(jnp.zeros((1, 128), F32))
        for e in range(8):
            tail = jnp.concatenate([lines_here[e], filler], axis=0)
            for target, half in ((keep, c), (send, 1 - c)):
                rows = pl.ds(pl.multiple_of(dest * 128 + half * 64 + e * 8, 8), 8)
                target[dest * 8 + e] = jnp.concatenate(
                    [grad_rows[rows, kind * 128 : kind * 128 + 128] for kind in range(3)]
                    + [out_rows[rows, cb * 128 : cb * 128 + 128] for cb in range(2)]
                    + [tail],
                    axis=0,
                ).astype(BF16)
    keep.send()
    send.send()
    dq_rows[...] = whole.T
    for k in range(4):
        base = lax.rem(z - k + 4, 4) * 256
        dq_keep[k * 128 : k * 128 + 128, :] = dq_rows[pl.ds(pl.multiple_of(base + xh * 128, 128), 128), :]
        theirs = pl.ds(pl.multiple_of(base + (1 - xh) * 128, 128), 128)
        for kind in range(3):
            at = kind * 512 + k * 128
            dq_send[at : at + 128, :] = dq_rows[theirs, kind * 128 : kind * 128 + 128]


def mlp_grad_kernel(ids, m0, m1, m2, m3, o0, o1, o2, o3, gate_up, down):
    c, y, xl = ids[ID_C], ids[ID_Y], ids[ID_XL]
    mine, other = (m0, m1, m2, m3), (o0, o1, o2, o3)
    zero = c == 0

    def place(k, i):
        return lax.rem(xl + i, 2), lax.rem(y - k + 4, 4)

    def wide(ref, i, z, which):
        at = z * 96 + which * 48
        return jnp.concatenate(
            [ref[i, at + cb * 16 : at + cb * 16 + 16, :].astype(F32) for cb in range(3)], axis=1
        )[:, :UNITS]

    for k in range(4):
        for i in range(2):
            to_xl, to_y = place(k, i)
            rows = pl.ds(pl.multiple_of(to_xl * 64 + to_y * 16, 16), 16)
            for which in range(2):
                parts = []
                for z in range(4):
                    a, b = wide(mine[k], i, z, which), wide(other[k], i, z, which)
                    parts += [jnp.where(zero, a, b), jnp.where(zero, b, a)]
                gate_up[rows, which * FF : which * FF + FF] = jnp.concatenate(parts, axis=1)
    gate_up.send()
    for refs, half in ((mine, c), (other, 1 - c)):
        for k in range(4):
            lanes = pl.ds(pl.multiple_of(half * 512 + place(k, 0)[1] * 128, 128), 128)
            down[:, lanes] = refs[k][0, 384:736, :].astype(F32) + refs[k][1, 384:736, :].astype(F32)


def qkv_grad_kernel(ids, mine, other, qkv, out_w, qkv_bias, attn_gain, attn_bias, mlp_gain, mlp_bias):
    c = ids[ID_C]
    s = ids[ID_Z] * 2 + ids[ID_XH]
    totals = []
    for ref, half in ((mine, c), (other, 1 - c)):
        for e in range(8):
            rows = pl.ds(pl.multiple_of(half * 64 + e * 8, 8), 8)
            tiles = [ref[e, src * 48 : src * 48 + 48, :].astype(F32) for src in range(8)]
            for src in range(8):
                for kind in range(3):
                    lanes = slice(kind * D + src * 128, kind * D + src * 128 + 128)
                    qkv[rows, lanes] = tiles[src][kind * 8 : kind * 8 + 8]
            for z in range(4):
                for cb in range(2):
                    lanes = slice(z * 256 + cb * 128, z * 256 + cb * 128 + 128)
                    at = slice(24 + cb * 8, 32 + cb * 8)
                    out_w[rows, lanes] = tiles[2 * z][at] + tiles[2 * z + 1][at]
            if ref is mine:
                totals.append([tile[40:41] for tile in tiles])
    for e, vector in enumerate((attn_gain, attn_bias, mlp_gain, mlp_bias)):
        total = totals[e][0]
        for line in totals[e][1:]:
            total = total + line
        vector[...] = total
    for i in range(3):
        block = 3 * s + i
        found = jnp.zeros((1, 128), F32)
        for src in range(8):
            for kind in range(3):
                found += jnp.where(block == 8 * kind + src, totals[4 + kind][src], 0.0)
        qkv_bias[:, i * 128 : i * 128 + 128] = found


def shards(
    block_input,
    attn_gain,
    attn_bias,
    query_key_value_weight,
    query_key_value_bias,
    output_projection_weight,
    mlp_gain,
    mlp_bias,
    gate_up_projection_weight,
    down_projection_weight,
    out_grad,
):
    y = lax.axis_index("y")
    c = lax.axis_index("c")
    z = lax.axis_index("z")
    xh = lax.axis_index("xh")
    xl = lax.axis_index("xl")
    ids = jnp.stack([y, c, z, xh, xl]).astype(jnp.int32)
    x_own = block_input[0]
    dy_own = out_grad[0]
    cos_np, sin_np = rotary_tables()
    cos, sin = jnp.asarray(cos_np), jnp.asarray(sin_np)

    gu_rows = lax.dynamic_slice_in_dim(gate_up_projection_weight, y * 32, 32, 0).reshape(32, 2, 4, 2, UNITS)
    gu_rows = lax.dynamic_index_in_dim(gu_rows, c, 3, keepdims=False)
    gu_rows = jnp.pad(gu_rows, ((0, 0), (0, 0), (0, 0), (0, PAD - UNITS))).reshape(32, 2, 4, 3, 128)
    gu_part = jnp.broadcast_to(gu_rows.transpose(2, 1, 3, 0, 4).reshape(4, 1, 192, 128), (4, 2, 192, 128))
    out_rows = lax.dynamic_slice(output_projection_weight, (y * 32, c * 512), (32, 512))
    out_part = out_rows.reshape(32, 4, 128).transpose(1, 0, 2).reshape(128, 128)
    tail = jnp.broadcast_to(out_part[None], (8, 128, 128))

    x_part = x_own.reshape(128, 8, 128).transpose(1, 0, 2).reshape(D, 128)
    vec = jnp.concatenate(
        [
            jnp.stack([attn_gain, attn_bias, mlp_gain, mlp_bias]),
            query_key_value_bias.reshape(3, 128),
            jnp.zeros((9, 128), BF16),
        ]
    )
    qkv_rows = lax.dynamic_slice_in_dim(query_key_value_weight, c * 64, 64, 0)
    qkv_part = qkv_rows.reshape(64, 3, 8, 128).transpose(2, 1, 0, 3).reshape(8, 192, 128)
    head = jnp.broadcast_to(jnp.concatenate([x_part, vec])[None], (8, QKV_AT, 128))
    packet = jnp.concatenate([head, qkv_part, gu_part.reshape(8, 192, 128), tail], axis=1)
    packet, down_now = tie(exchange(packet, SHARD), down_projection_weight)
    down_other = swap(down_now, "xh")
    piece = packet[:, GU_AT:]
    before, after = turn(piece, "y", 1), turn(piece, "y", 3)
    qkv_other = swap(packet[:, QKV_AT:GU_AT], "c")
    head_of = lambda array: Part(array, 1, (8, GU_AT, 128), lambda ref, ids: [ref.at[:, 0:GU_AT]])
    qkv_t, att_blocks, lse, w_t = call(
        attend_kernel,
        "attend_forward",
        (shape(384, SEQ), shape(8, 512, 128), shape(8, SEQ, dtype=F32), shape(384, D)),
        (ids, head_of(packet), qkv_other, cos, sin),
        scratch=[pltpu.VMEM((D, 384), BF16)],
    )
    att_blocks, packet_late, far, dy_now = tie(att_blocks, packet, piece, dy_own)
    pieces = [piece, before, turn(far, "y", 2), after]
    dys = [dy_now] + [turn(dy_now, "z", k) for k in (1, 2, 3)]
    att = exchange(att_blocks, SHARD)
    (xhat,) = call(
        normed_kernel,
        "normed_input",
        (shape(SEQ, D),),
        (ids, Part(packet_late, 1, (8, D, 128), lambda ref, ids: [ref.at[:, 0:D]])),
    )
    pieces += [swap(p, "c") for p in pieces]
    gate_w, up_w, out_w = call(
        weights_kernel,
        "weights",
        (shape(D, 2 * PAD), shape(D, 2 * PAD), shape(D, D)),
        (ids, *pieces),
    )

    vecs = packet[:, VEC_AT : VEC_AT + 4].astype(F32).transpose(1, 0, 2).reshape(4, 1, D)
    gain_one, bias_one, gain_two, bias_two = vecs[0], vecs[1], vecs[2], vecs[3]
    out_w, xhat = tie(out_w, xhat)
    w_t_other = swap(w_t, "xh")

    mixed_own, att_rel, mlp_small, ds, keep, send, *outs = call(
        mlp_kernel,
        "mlp",
        (
            shape(128, D, dtype=F32),
            shape(512, D),
            shape(8, D, dtype=F32),
            shape(4, 128, D),
            shape(4, 2240, 128),
            shape(4, 2240, 128),
        )
        + (shape(128, D),) * 4,
        (
            ids,
            out_w,
            att,
            Part(
                packet,
                4,
                (D, 128),
                lambda ref, ids: [ref.at[2 * lax.rem(ids[ID_Z] - k + 4, 4) + ids[ID_XH], 0:D] for k in range(4)],
            ),
            gate_w,
            up_w,
            gain_two,
            bias_two,
            *dys,
            down_projection_weight,
            down_other,
        ),
        scratch=[pltpu.VMEM((2 * PAD, D), BF16), pltpu.VMEM((512, D), BF16)]
        + [pltpu.VMEM((512, 2 * PAD), BF16)] * 3
        + [pltpu.VMEM((2 * PAD, D), BF16)],
    )
    ds = exchange(ds, "z")
    mlp_chunks = (keep.astype(F32) + swap(send, "c").astype(F32)).astype(BF16)
    dmixed, blocks = call(
        norm_kernel,
        "norm_backward",
        (shape(128, D, dtype=F32), shape(8, 384, 128)),
        (ids, ds, dy_own, mixed_own, gain_two, out_w),
    )
    blocks = exchange(blocks, SHARD)

    mlp_y = mlp_chunks[0].astype(F32)
    for k in (1, 2, 3):
        mlp_y = mlp_y + turn(mlp_chunks[k], "y", -k).astype(F32)
    mlp_y = mlp_y.astype(BF16)

    grad_keep, grad_send, dq_keep, dq_send = call(
        attend_back_kernel,
        "attend_backward",
        (shape(64, 48, 128), shape(64, 48, 128), shape(512, 384), shape(1536, 128)),
        (ids, blocks, qkv_t, lse, cos, sin, xhat, w_t, gain_one, bias_one, mlp_small, att_rel),
        scratch=[
            pltpu.VMEM((SEQ, HEAD_DIM), F32),
            pltpu.VMEM((SEQ, HEAD_DIM), F32),
            pltpu.VMEM((384, SEQ), BF16),
            pltpu.VMEM((SEQ, 384), BF16),
            pltpu.VMEM((D, 384), F32),
            pltpu.VMEM((D, 256), F32),
        ],
    )

    gu_recv = exchange(mlp_y[:1536].reshape(16, 96, 128), ("z", "xh", "xl"))
    grad_send, gu_recv, w_t_other = tie(grad_send, gu_recv, w_t_other)
    chunks = (grad_keep.astype(F32) + swap(grad_send, "c").astype(F32)).astype(BF16)
    chunks, dq_send = tie(chunks, dq_send)
    both = swap(jnp.concatenate([dq_send, mlp_y[1888:2240]], axis=0), "xh")
    dq_recv = both[:1536].reshape(3, 512, 128)
    do_piece = (mlp_y[1536:1888].astype(F32) + both[1536:].astype(F32)).astype(BF16)
    chunks = exchange(chunks, ("z", "xh", "xl", "y"))
    grad_piece = jnp.sum(chunks.reshape(8, 8, 48, 128).astype(F32), axis=1).astype(BF16).reshape(384, 128)
    gu_piece = jnp.sum(gu_recv.reshape(4, 4, 96, 128).astype(F32), axis=1).astype(BF16).reshape(384, 128)
    mlp_piece = jnp.concatenate([gu_piece, do_piece], axis=0)
    grad_piece, mlp_far = tie(grad_piece, swap(mlp_piece, "xl"))
    mlp_pair = jnp.stack([mlp_piece, mlp_far])
    mlp_near = [mlp_pair] + [turn(mlp_pair, "y", k) for k in (1, 2, 3)]
    dfirst_part = (dot(dq_keep, w_t) + dot(jnp.concatenate(list(dq_recv), axis=1), w_t_other)).astype(BF16)
    parts = [jnp.concatenate([outs[k], dfirst_part[k * 128 : k * 128 + 128]], axis=0) for k in range(4)]
    parts = [parts[0]] + [turn(parts[k], "z", -k) for k in (1, 2, 3)]
    mine = spread(grad_piece, PLANE, 8)
    total = sum(part.astype(F32) for part in parts)
    block_output = (mixed_own + total[:128]).astype(BF16)[None]
    normed_one, inverse_one = normalize(x_own.astype(F32))
    input_grad = (dmixed + norm_back(total[128:] * gain_one, normed_one, inverse_one)).astype(BF16)[None]

    gate_up_grad, down_grad = call(
        mlp_grad_kernel,
        "mlp_grad",
        (shape(128, 2 * FF, dtype=F32), shape(UNITS, D, dtype=F32)),
        (ids, *mlp_near, *[swap(value, "c") for value in mlp_near]),
    )

    qkv_grad, out_w_grad, qkv_bias_grad, *vectors = call(
        qkv_grad_kernel,
        "qkv_grad",
        (shape(128, 3 * D, dtype=F32), shape(128, D, dtype=F32), shape(1, 384, dtype=F32))
        + (shape(1, 128, dtype=F32),) * 4,
        (ids, mine, swap(mine, "c")),
    )
    vectors = [vector.reshape(128) for vector in vectors]

    return (
        block_output,
        input_grad,
        vectors[0],
        vectors[1],
        qkv_grad,
        qkv_bias_grad.reshape(384),
        out_w_grad,
        vectors[2],
        vectors[3],
        gate_up_grad,
        down_grad,
    )


def solution(mesh):
    fine = jax.sharding.Mesh(mesh.devices.reshape(2, 4, 2, 4, 2), ("xl", "y", "c", "z", "xh"))
    tokens = P(("xl", "y", "c"), SHARD, None)
    rows = P(SHARD, None)
    flat = P(SHARD)
    return jax.shard_map(
        shards,
        mesh=fine,
        in_specs=(tokens, flat, flat, rows, flat, rows, flat, flat, rows, rows, tokens),
        out_specs=(tokens, tokens, flat, flat, rows, flat, rows, flat, flat, rows, rows),
        check_vma=False,
    )
```

```python
import jax
import jax.numpy as jnp
import numpy as np
from jax import lax
from jax.experimental import pallas as pl
from jax.experimental.pallas import tpu as pltpu
from jax.sharding import PartitionSpec as P

D = 1024
HEADS = 16
HEAD_DIM = 64
FF = 2816
ROTARY = 16
SEQ = 1024
BLOCK = 256
UNITS = 352
PAD = 384

EPSILON = 1e-05
SCORE_SCALE = 0.125

SHARD = ("z", "xh")
PLANE = ("xl", "y")
F32 = jnp.float32
BF16 = jnp.bfloat16
MIB = 1024 * 1024

VEC_AT, QKV_AT, GU_AT = 1024, 1040, 1232


def normalize(values):
    center = values - jnp.mean(values, axis=-1, keepdims=True)
    variance = jnp.mean(center * center, axis=-1, keepdims=True)
    inverse = lax.rsqrt(variance + EPSILON)
    return (center * inverse, inverse)


def norm_back(scaled_grad, normed, inverse):
    return inverse * (
        scaled_grad
        - jnp.mean(scaled_grad, axis=-1, keepdims=True)
        - normed * jnp.mean(scaled_grad * normed, axis=-1, keepdims=True)
    )


def rotary_tables():
    half = ROTARY // 2
    frequency = np.float32(10000.0) ** (-np.arange(half, dtype=np.float32) * np.float32(2.0) / np.float32(ROTARY))
    angles = np.arange(SEQ, dtype=np.float32)[None, :] * frequency.astype(np.float32)[:, None]
    return np.cos(angles).astype(np.float32), np.sin(angles).astype(np.float32)


def exchange(value, axes):
    return lax.all_to_all(value, axes, 0, 0, tiled=True)


def spread(value, axes, count):
    return exchange(jnp.broadcast_to(value[None], (count,) + value.shape), axes)


def swap(value, axis):
    return lax.ppermute(value, axis, [(0, 1), (1, 0)])


def turn(value, axis, step):
    return lax.ppermute(value, axis, [(i, (i + step) % 4) for i in range(4)])


def index_of(xl, y, c, z, xh):
    return (((xl * 4 + y) * 2 + c) * 4 + z) * 2 + xh


def move(value, target):
    pairs = []
    for xl in range(2):
        for y in range(4):
            for c in range(2):
                for z in range(4):
                    for xh in range(2):
                        pairs.append((index_of(xl, y, c, z, xh), index_of(*target(xl, y, c, z, xh))))
    return lax.ppermute(value, ("xl", "y", "c", "z", "xh"), pairs)


def tie(*values):
    return lax.optimization_barrier(values)


def dot(a, b, dims=((1,), (0,))):
    return lax.dot_general(a, b, (dims, ((), ())), preferred_element_type=F32)


NT = ((1,), (1,))

ID_Y, ID_C, ID_Z, ID_XH, ID_XL = range(5)


class Part:
    def __init__(self, array, count, dims, views):
        self.array, self.shape, self.dtype, self.views = array, (count,) + dims, array.dtype, views


class Later:
    def __init__(self, copies, buffer):
        self.copies, self.buffer = copies, buffer

    def arrive(self):
        for copy in self.copies:
            copy.wait()
        self.copies = []
        return self.buffer

    def __getitem__(self, index):
        return self.arrive()[index]


class Result:
    def __init__(self, copy, buffer):
        self.copy, self.buffer, self.sent = copy, buffer, False

    def __setitem__(self, index, value):
        self.buffer[index] = value

    def __getitem__(self, index):
        return self.buffer[index]

    def send(self):
        if not self.sent:
            self.copy.start()
            self.sent = True


def call(kernel, name, out_shape, args, scratch=(), moved=1):
    count, outs, own = len(args) - 1, len(out_shape), len(scratch)

    def body(ids, *refs):
        sources, rest = refs[:count], refs[count:]
        targets, mine, rest = rest[:outs], rest[outs : outs + own], rest[outs + own :]
        buffers, results, (sems, out_sems) = rest[:count], rest[count:-2], rest[-2:]
        inputs = []
        at = 0
        for i in range(count):
            if isinstance(args[i + 1], Part):
                views = args[i + 1].views(sources[i], ids)
                copies = [
                    pltpu.make_async_copy(view, buffers[i].at[j], sems.at[at + j]) for j, view in enumerate(views)
                ]
            else:
                copies = [pltpu.make_async_copy(sources[i], buffers[i], sems.at[at])]
            at += len(copies)
            for copy in copies:
                copy.start()
            inputs.append(Later(copies, buffers[i]))
        outputs = [
            Result(pltpu.make_async_copy(results[i], targets[i], out_sems.at[i]), results[i]) for i in range(outs)
        ]
        kernel(ids, *inputs, *outputs, *mine)
        for value in inputs:
            value.arrive()
        for value in outputs:
            value.send()
        for value in outputs:
            value.copy.wait()

    flights = sum(a.shape[0] if isinstance(a, Part) else 1 for a in args[1:])
    return pl.pallas_call(
        body,
        out_shape=out_shape,
        in_specs=[pl.BlockSpec(memory_space=pltpu.SMEM)] + [pl.BlockSpec(memory_space=pltpu.HBM)] * count,
        out_specs=tuple(pl.BlockSpec(memory_space=pltpu.HBM) for _ in out_shape),
        scratch_shapes=list(scratch)
        + [pltpu.VMEM(a.shape, a.dtype) for a in list(args[1:]) + list(out_shape)]
        + [pltpu.SemaphoreType.DMA((flights,)), pltpu.SemaphoreType.DMA((outs,))],
        compiler_params=pltpu.CompilerParams(vmem_limit_bytes=60 * MIB),
        cost_estimate=pl.CostEstimate(flops=0, bytes_accessed=moved, transcendentals=0),
        name=name,
    )(*[a.array if isinstance(a, Part) else a for a in args])


def shape(*dims, dtype=BF16):
    return jax.ShapeDtypeStruct(dims, dtype)


def turned(value, cos, sin, sign):
    a = value[0:8]
    b = value[8:16]
    return jnp.concatenate([a * cos - sign * (b * sin), b * cos + sign * (a * sin), value[16:]], axis=0)


def qkv_weights(c, packet, other, w_rows, w_out):
    mine = pl.multiple_of(c * 64, 64)
    theirs = pl.multiple_of((1 - c) * 64, 64)
    for src in range(8):
        for kind in range(3):
            lanes = slice(kind * 128, kind * 128 + 128)
            at = QKV_AT + kind * 64
            w_rows[pl.ds(src * 128 + mine, 64), lanes] = packet[0, src, at : at + 64, :]
            w_rows[pl.ds(src * 128 + theirs, 64), lanes] = other[src, kind * 64 : kind * 64 + 64, :]
    for kind in range(3):
        for src in range(8):
            w_out[kind * 128 : kind * 128 + 128, src * 128 : src * 128 + 128] = w_rows[
                src * 128 : src * 128 + 128, kind * 128 : kind * 128 + 128
            ].T


def normed_kernel(ids, packet, xhat_out):
    for block in range(8):
        x = jnp.concatenate([packet[0, block, cb * 128 : cb * 128 + 128, :].astype(F32) for cb in range(8)], axis=1)
        xhat_out[block * 128 : block * 128 + 128, :] = normalize(x)[0].astype(BF16)


def attend_kernel(ids, packet, other, cos_ref, sin_ref, qkv_out, attended, lse_out, w_out, w_rows):
    c = ids[ID_C]
    s = ids[ID_Z] * 2 + ids[ID_XH]
    qkv_weights(c, packet, other, w_rows, w_out)
    w_out.send()
    vec = [packet[0, src, VEC_AT : VEC_AT + 16, :].astype(F32) for src in range(8)]
    gain = jnp.concatenate([v[0:1] for v in vec], axis=1)
    bias = jnp.concatenate([v[1:2] for v in vec], axis=1)
    row = lax.broadcasted_iota(jnp.int32, (16, 128), 0)
    qkv_bias = []
    for kind in range(3):
        total = jnp.zeros((16, 128), F32)
        for src in range(8):
            total += jnp.where((row >= 4) & (row < 7) & (row - 4 + 3 * src == 8 * kind + s), vec[src], 0.0)
        line = jnp.sum(total, axis=0, keepdims=True)
        qkv_bias.append(jnp.broadcast_to(line, (128, 128)).T)
    qkv_bias = jnp.concatenate(qkv_bias, axis=0)
    qkv_bias = jnp.concatenate([qkv_bias, qkv_bias], axis=1)
    for block in range(SEQ // BLOCK):
        lo = block * BLOCK
        x = jnp.concatenate(
            [
                jnp.concatenate(
                    [packet[0, 2 * block + i, cb * 128 : cb * 128 + 128, :].astype(F32) for cb in range(8)], axis=1
                )
                for i in range(2)
            ],
            axis=0,
        )
        normed, _ = normalize(x)
        first_in = (normed * gain + bias).astype(BF16)
        part = dot(w_out[...], first_in, NT) + qkv_bias
        cos = cos_ref[:, lo : lo + BLOCK]
        sin = sin_ref[:, lo : lo + BLOCK]
        for kind in range(3):
            for head in range(2):
                base = kind * 128 + head * 64
                full = part[base : base + 64]
                if kind < 2:
                    full = turned(full, cos, sin, 1.0)
                qkv_out[base : base + 64, lo : lo + BLOCK] = full.astype(BF16)
    qkv_out.send()
    row = lax.broadcasted_iota(jnp.int32, (BLOCK, BLOCK), 0)
    col = lax.broadcasted_iota(jnp.int32, (BLOCK, BLOCK), 1)
    lse_out[...] = jnp.zeros((8, SEQ), F32)
    for block in range(SEQ // BLOCK):
        lo = block * BLOCK
        hi = lo + BLOCK
        both = []
        for head in range(2):
            keys = qkv_out[128 + head * 64 : 128 + head * 64 + 64, :hi].T
            value_t = qkv_out[256 + head * 64 : 256 + head * 64 + 64, :hi]
            query_t = qkv_out[head * 64 : head * 64 + 64, lo:hi] * jnp.bfloat16(SCORE_SCALE)
            parts = []
            if block:
                parts.append(dot(keys[:lo], query_t))
            parts.append(jnp.where(row <= col, dot(keys[lo:hi], query_t), -jnp.inf))
            scores = jnp.concatenate(parts, axis=0) if block else parts[0]
            top = jnp.max(scores, axis=0, keepdims=True)
            exps = jnp.exp(scores - top)
            total = jnp.sum(exps, axis=0, keepdims=True)
            both.append(dot(value_t, exps.astype(BF16)) / total)
            lse_out[head : head + 1, lo:hi] = top + jnp.log(total)
        out = jnp.concatenate(both, axis=0).T.astype(BF16)
        for parity in range(2):
            for zt in range(4):
                attended[2 * zt + parity, block * 128 : block * 128 + 128, :] = out[parity * 128 : parity * 128 + 128]


def weights_kernel(ids, p0, p1, p2, p3, p4, p5, p6, p7, gate_w, up_w, out_w):
    y, c = ids[ID_Y], ids[ID_C]
    for k, refs in enumerate(((p0, p4), (p1, p5), (p2, p6), (p3, p7))):
        at = pl.multiple_of(lax.rem(y - k + 4, 4) * 32, 32)
        for core, ref in enumerate(refs):
            half = c if core == 0 else 1 - c
            for src in range(8):
                rows = pl.ds(src * 128 + at, 32)
                for cb in range(3):
                    lanes = slice(core * PAD + cb * 128, core * PAD + cb * 128 + 128)
                    gate_w[rows, lanes] = ref[src, cb * 32 : cb * 32 + 32, :]
                    up_w[rows, lanes] = ref[src, 96 + cb * 32 : 96 + cb * 32 + 32, :]
                for cb in range(4):
                    lanes = pl.ds(pl.multiple_of(half * 512 + cb * 128, 128), 128)
                    out_w[rows, lanes] = ref[src, 192 + cb * 32 : 192 + cb * 32 + 32, :]


def assemble_down(ids, own, other, down_w):
    swapped = jnp.where(ids[ID_XH] == ids[ID_C], 0, PAD)
    down_w[pl.ds(pl.multiple_of(swapped, 128), UNITS), :] = own[...]
    down_w[pl.ds(pl.multiple_of(PAD - swapped, 128), UNITS), :] = other[...]
    for base in (UNITS, PAD + UNITS):
        down_w[base : base + PAD - UNITS, :] = jnp.zeros((PAD - UNITS, D), BF16)


def cotangent(parts):
    return jnp.concatenate([part[...] for part in parts], axis=0)


def mlp_kernel(
    ids, out_w, att, x_ref, gate_w, up_w, gain_ref, bias_ref, dy0, dy1, dy2, dy3, down_own, down_other, mixed_own, att_out, small, ds, keep, send, out0, out1, out2, out3, down_w, second_out, hidden_out, dgate_out, dup_out, held
):
    z = ids[ID_Z]
    gain = gain_ref[...]
    bias = bias_ref[...]
    gain_sum = jnp.zeros((1, D), F32)
    bias_sum = jnp.zeros((1, D), F32)
    for pair in range(2):
        rows = slice(pair * 256, pair * 256 + 256)
        a_parts = []
        x_parts = []
        for k in (2 * pair, 2 * pair + 1):
            place = lax.rem(z - k + 4, 4)
            at = pl.ds(pl.multiple_of(place * 128, 128), 128)
            a_parts.append(jnp.concatenate([att[src, at, :] for src in range(8)], axis=1))
            x_parts.append(
                jnp.concatenate([x_ref[k, cb * 128 : cb * 128 + 128, :] for cb in range(8)], axis=1)
            )
        attended = jnp.concatenate(a_parts, axis=0)
        att_out[rows, :] = attended
        mixed = jnp.concatenate(x_parts, axis=0).astype(F32) + dot(attended, out_w[...])
        if pair == 0:
            mixed_own[...] = mixed[:128]
        normed, _ = normalize(mixed)
        second_in = (normed * gain + bias).astype(BF16)
        second_out[rows, :] = second_in
        gate = dot(second_in, gate_w[...])
        up_part = dot(second_in, up_w[...])
        sig = jax.nn.sigmoid(gate)
        silu = gate * sig
        hidden_out[rows, :] = (silu * up_part).astype(BF16)
        dy = cotangent((dy0, dy1, dy2, dy3)[2 * pair : 2 * pair + 2])
        if pair == 0:
            assemble_down(ids, down_own, down_other, down_w)
        dhidden = dot(dy, down_w[...], NT)
        dgate = (dhidden * up_part * sig * (1.0 + gate * (1.0 - sig))).astype(BF16)
        dup = (dhidden * silu).astype(BF16)
        dgate_out[rows, :] = dgate
        dup_out[rows, :] = dup
        dsecond = dot(dgate, gate_w[...], NT) + dot(dup, up_w[...], NT)
        gain_sum += jnp.sum(dsecond * normed, axis=0, keepdims=True)
        bias_sum += jnp.sum(dsecond, axis=0, keepdims=True)
        low = dsecond.astype(BF16)
        for i in range(2):
            ds[lax.rem(z - (2 * pair + i) + 4, 4)] = low[i * 128 : i * 128 + 128]
    small[...] = jnp.concatenate([gain_sum, bias_sum, jnp.zeros((6, D), F32)], axis=0)
    ds.send()
    att_out.send()

    y, c, xh, xl = ids[ID_Y], ids[ID_C], ids[ID_XH], ids[ID_XL]

    def place(to_y):
        return lax.rem(y - to_y + 4, 4)

    for block in range(4):
        turned_in = second_out[:, block * 256 : block * 256 + 256].T
        for which, grad in ((0, dgate_out), (1, dup_out)):
            part = dot(turned_in, grad[...]).astype(BF16)
            for target, base in ((keep, 0), (send, PAD)):
                for i in range(16):
                    owner, to_xl, to_y = block * 2 + i // 8, (i // 4) % 2, i % 4
                    for cb in range(3):
                        at = (owner * 2 + to_xl) * 96 + (which * 3 + cb) * 16
                        target[place(to_y), at : at + 16, :] = part[
                            i * 16 : i * 16 + 16, base + cb * 128 : base + cb * 128 + 128
                        ]
    hidden_t = hidden_out[...].T
    held[...] = dot(hidden_t, cotangent((dy0, dy1, dy2, dy3))).astype(BF16)
    for target, half in ((keep, c), (send, 1 - c)):
        for base, to_xh in ((0, c), (PAD, 1 - c)):
            for to_xl in range(2):
                rows = pl.ds(pl.multiple_of(1536 + jnp.abs(xh - to_xh) * 352 + to_xl * 176, 16), 176)
                for cb in range(4):
                    lanes = pl.ds(pl.multiple_of(half * 512 + cb * 128, 128), 128)
                    target[place(cb), rows, :] = held[base + to_xl * 176 : base + to_xl * 176 + 176, lanes]
    send.send()
    keep.send()
    for pair in range(2):
        part = dot(hidden_out[pair * 256 : pair * 256 + 256, :], down_w[...]).astype(BF16)
        ((out0, out1), (out2, out3))[pair][0][...] = part[:128]
        ((out0, out1), (out2, out3))[pair][1][...] = part[128:]


def norm_kernel(ids, ds, dy, mixed_ref, gain_ref, out_w, dmixed_out, blocks):
    dsecond = ds[0].astype(F32) + ds[1].astype(F32) + ds[2].astype(F32) + ds[3].astype(F32)
    normed, inverse = normalize(mixed_ref[...])
    dmixed = dy[...].astype(F32) + norm_back(dsecond * gain_ref[...], normed, inverse)
    dmixed_out[...] = dmixed
    dproj = dmixed.astype(BF16)
    dattended = dot(dproj, out_w[...], NT).astype(BF16)
    for dest in range(8):
        blocks[dest, :128, :] = dattended[:, dest * 128 : dest * 128 + 128]
        for cb in range(2):
            at = (dest // 2) * 256 + cb * 128
            blocks[dest, 128 + cb * 128 : 256 + cb * 128, :] = dproj[:, at : at + 128]


def attend_back_kernel(
    ids, blocks, qkv, lse_ref, cos_ref, sin_ref, xhat, w_t, gain_ref, bias_ref, small, att, keep, send, dq_keep,
    dq_send, dkey, dvalue, dq_t, dq_rows, grad_rows, out_rows
):
    c, z, xh = ids[ID_C], ids[ID_Z], ids[ID_XH]
    cos = cos_ref[...]
    sin = sin_ref[...]
    row = lax.broadcasted_iota(jnp.int32, (BLOCK, BLOCK), 0)
    col = lax.broadcasted_iota(jnp.int32, (BLOCK, BLOCK), 1)
    for head in range(2):
        dkey[...] = jnp.zeros_like(dkey)
        dvalue[...] = jnp.zeros_like(dvalue)
        key_t = qkv[128 + head * 64 : 128 + head * 64 + 64, :]
        keys = key_t.T
        values = qkv[256 + head * 64 : 256 + head * 64 + 64, :].T
        dquery = []
        for block in range(SEQ // BLOCK):
            lo = block * BLOCK
            hi = lo + BLOCK
            query_t = qkv[head * 64 : head * 64 + 64, lo:hi] * jnp.bfloat16(SCORE_SCALE)
            query = query_t.T
            grad = jnp.concatenate(
                [blocks[2 * block + i, :128, head * 64 : head * 64 + 64] for i in range(2)], axis=0
            )
            grad_t = grad.T
            lse = lse_ref[head : head + 1, lo:hi]
            parts = []
            if block:
                parts.append(jnp.exp(dot(keys[:lo], query_t) - lse))
            parts.append(jnp.where(row <= col, jnp.exp(dot(keys[lo:hi], query_t) - lse), 0.0))
            shares = jnp.concatenate(parts, axis=0) if block else parts[0]
            dshares = dot(values[:hi], grad_t)
            row_dot = jnp.sum(shares * dshares, axis=0, keepdims=True)
            dscores = (shares * (dshares - row_dot)).astype(BF16)
            dvalue[:hi] += dot(shares.astype(BF16), grad)
            dkey[:hi] += dot(dscores, query)
            dquery.append(dot(key_t[:, :hi], dscores) * SCORE_SCALE)
        dquery_t = jnp.concatenate(dquery, axis=1)
        dq_t[head * 64 : head * 64 + 64, :] = turned(dquery_t, cos, sin, -1.0).astype(BF16)
        dq_t[128 + head * 64 : 128 + head * 64 + 64, :] = turned(dkey[...].T, cos, sin, -1.0).astype(BF16)
        dq_t[256 + head * 64 : 256 + head * 64 + 64, :] = dvalue[...].T.astype(BF16)
    whole = dq_t[...]
    sums = jnp.sum(whole.astype(F32), axis=1, keepdims=True)
    product = dot(whole, xhat[...])
    weights = w_t[...].astype(F32)
    gain_part = jnp.sum(product * weights, axis=0, keepdims=True)
    bias_part = jnp.sum(sums * weights, axis=0, keepdims=True)
    grad_rows[...] = (product * gain_ref[...] + sums * bias_ref[...]).T
    dproj = jnp.concatenate(
        [
            jnp.concatenate(
                [blocks[2 * lax.rem(z - k + 4, 4) + xh, 128 + cb * 128 : 256 + cb * 128, :] for cb in range(2)], axis=1
            )
            for k in range(4)
        ],
        axis=0,
    )
    for block in range(4):
        rows = slice(block * 256, block * 256 + 256)
        out_rows[rows, :] = dot(att[:, rows].T, dproj)
    lines = [
        jnp.broadcast_to(sums[kind * 128 : kind * 128 + 128], (128, 128)).T[0:1] for kind in range(3)
    ]
    filler = jnp.zeros((7, 128), F32)
    for dest in range(8):
        lanes = slice(dest * 128, dest * 128 + 128)
        lines_here = [gain_part[:, lanes], bias_part[:, lanes], small[0:1, lanes], small[1:2, lanes]] + lines
        lines_here.append(jnp.zeros((1, 128), F32))
        for e in range(8):
            tail = jnp.concatenate([lines_here[e], filler], axis=0)
            for target, half in ((keep, c), (send, 1 - c)):
                rows = pl.ds(pl.multiple_of(dest * 128 + half * 64 + e * 8, 8), 8)
                target[dest * 8 + e] = jnp.concatenate(
                    [grad_rows[rows, kind * 128 : kind * 128 + 128] for kind in range(3)]
                    + [out_rows[rows, cb * 128 : cb * 128 + 128] for cb in range(2)]
                    + [tail],
                    axis=0,
                ).astype(BF16)
    keep.send()
    send.send()
    dq_rows[...] = whole.T
    for k in range(4):
        base = lax.rem(z - k + 4, 4) * 256
        dq_keep[k * 128 : k * 128 + 128, :] = dq_rows[pl.ds(pl.multiple_of(base + xh * 128, 128), 128), :]
        theirs = pl.ds(pl.multiple_of(base + (1 - xh) * 128, 128), 128)
        for kind in range(3):
            at = kind * 512 + k * 128
            dq_send[at : at + 128, :] = dq_rows[theirs, kind * 128 : kind * 128 + 128]


def mlp_grad_kernel(ids, m0, m1, m2, m3, o0, o1, o2, o3, gate_up, down):
    c, y, xl = ids[ID_C], ids[ID_Y], ids[ID_XL]
    mine, other = (m0, m1, m2, m3), (o0, o1, o2, o3)
    zero = c == 0

    def place(k, i):
        return lax.rem(xl + i, 2), lax.rem(y - k + 4, 4)

    def wide(ref, i, z, which):
        at = i * 384 + z * 96 + which * 48
        return jnp.concatenate(
            [ref[at + cb * 16 : at + cb * 16 + 16, :].astype(F32) for cb in range(3)], axis=1
        )[:, :UNITS]

    for k in range(4):
        for i in range(2):
            to_xl, to_y = place(k, i)
            rows = pl.ds(pl.multiple_of(to_xl * 64 + to_y * 16, 16), 16)
            for which in range(2):
                parts = []
                for z in range(4):
                    a, b = wide(mine[k], i, z, which), wide(other[k], i, z, which)
                    parts += [jnp.where(zero, a, b), jnp.where(zero, b, a)]
                gate_up[rows, which * FF : which * FF + FF] = jnp.concatenate(parts, axis=1)
    gate_up.send()
    for refs, half in ((mine, c), (other, 1 - c)):
        for k in range(4):
            lanes = pl.ds(pl.multiple_of(half * 512 + place(k, 0)[1] * 128, 128), 128)
            down[:, lanes] = refs[k][768:1120, :].astype(F32)


def last_kernel(ids, mine, other, qkv, out_w, qkv_bias, attn_gain, attn_bias, mlp_gain, mlp_bias):
    c = ids[ID_C]
    s = ids[ID_Z] * 2 + ids[ID_XH]
    totals = []
    for ref, half in ((mine, c), (other, 1 - c)):
        for e in range(8):
            rows = pl.ds(pl.multiple_of(half * 64 + e * 8, 8), 8)
            tiles = [ref[e, src * 48 : src * 48 + 48, :].astype(F32) for src in range(8)]
            for src in range(8):
                for kind in range(3):
                    lanes = slice(kind * D + src * 128, kind * D + src * 128 + 128)
                    qkv[rows, lanes] = tiles[src][kind * 8 : kind * 8 + 8]
            for z in range(4):
                for cb in range(2):
                    lanes = slice(z * 256 + cb * 128, z * 256 + cb * 128 + 128)
                    at = slice(24 + cb * 8, 32 + cb * 8)
                    out_w[rows, lanes] = tiles[2 * z][at] + tiles[2 * z + 1][at]
            if ref is mine:
                totals.append([tile[40:41] for tile in tiles])
    for e, vector in enumerate((attn_gain, attn_bias, mlp_gain, mlp_bias)):
        total = totals[e][0]
        for line in totals[e][1:]:
            total = total + line
        vector[...] = total
    for i in range(3):
        block = 3 * s + i
        found = jnp.zeros((1, 128), F32)
        for src in range(8):
            for kind in range(3):
                found += jnp.where(block == 8 * kind + src, totals[4 + kind][src], 0.0)
        qkv_bias[i * 128 : i * 128 + 128] = found.reshape(128)


def shards(
    block_input,
    attn_gain,
    attn_bias,
    query_key_value_weight,
    query_key_value_bias,
    output_projection_weight,
    mlp_gain,
    mlp_bias,
    gate_up_projection_weight,
    down_projection_weight,
    out_grad,
):
    y = lax.axis_index("y")
    c = lax.axis_index("c")
    z = lax.axis_index("z")
    xh = lax.axis_index("xh")
    xl = lax.axis_index("xl")
    ids = jnp.stack([y, c, z, xh, xl]).astype(jnp.int32)
    x_own = block_input[0]
    dy_own = out_grad[0]
    cos_np, sin_np = rotary_tables()
    cos, sin = jnp.asarray(cos_np), jnp.asarray(sin_np)

    gu_rows = lax.dynamic_slice_in_dim(gate_up_projection_weight, y * 32, 32, 0).reshape(32, 2, 4, 2, UNITS)
    gu_rows = lax.dynamic_index_in_dim(gu_rows, c, 3, keepdims=False)
    gu_rows = jnp.pad(gu_rows, ((0, 0), (0, 0), (0, 0), (0, PAD - UNITS))).reshape(32, 2, 4, 3, 128)
    gu_part = jnp.broadcast_to(gu_rows.transpose(2, 1, 3, 0, 4).reshape(4, 1, 192, 128), (4, 2, 192, 128))
    out_rows = lax.dynamic_slice(output_projection_weight, (y * 32, c * 512), (32, 512))
    out_part = out_rows.reshape(32, 4, 128).transpose(1, 0, 2).reshape(128, 128)
    tail = jnp.broadcast_to(out_part[None], (8, 128, 128))

    x_part = x_own.reshape(128, 8, 128).transpose(1, 0, 2).reshape(D, 128)
    vec = jnp.concatenate(
        [
            jnp.stack([attn_gain, attn_bias, mlp_gain, mlp_bias]),
            query_key_value_bias.reshape(3, 128),
            jnp.zeros((9, 128), BF16),
        ]
    )
    qkv_rows = lax.dynamic_slice_in_dim(query_key_value_weight, c * 64, 64, 0)
    qkv_part = qkv_rows.reshape(64, 3, 8, 128).transpose(2, 1, 0, 3).reshape(8, 192, 128)
    head = jnp.broadcast_to(jnp.concatenate([x_part, vec])[None], (8, QKV_AT, 128))
    packet = jnp.concatenate([head, qkv_part, gu_part.reshape(8, 192, 128), tail], axis=1)
    packet, down_now = tie(exchange(packet, SHARD), down_projection_weight)
    down_other = swap(down_now, "xh")
    piece = packet[:, GU_AT:]
    before, after = turn(piece, "y", 1), turn(piece, "y", 3)
    qkv_other = swap(packet[:, QKV_AT:GU_AT], "c")
    head_of = lambda array: Part(array, 1, (8, GU_AT, 128), lambda ref, ids: [ref.at[:, 0:GU_AT]])
    qkv_t, att_blocks, lse, w_t = call(
        attend_kernel,
        "attend_forward",
        (shape(384, SEQ), shape(8, 512, 128), shape(8, SEQ, dtype=F32), shape(384, D)),
        (ids, head_of(packet), qkv_other, cos, sin),
        scratch=[pltpu.VMEM((D, 384), BF16)],
    )
    att_blocks, packet_late, dy_now, far = tie(att_blocks, packet, dy_own, piece)
    att = exchange(att_blocks, SHARD)
    dy_now, before, after, down_other = tie(dy_now, before, after, down_other)
    dys = [dy_now] + [turn(dy_now, "z", k) for k in (1, 2, 3)]
    pieces = [piece, before, turn(far, "y", 2), after]
    (xhat,) = call(
        normed_kernel,
        "normed_input",
        (shape(SEQ, D),),
        (ids, Part(packet_late, 1, (8, D, 128), lambda ref, ids: [ref.at[:, 0:D]])),
    )
    pieces += [swap(p, "c") for p in pieces]
    gate_w, up_w, out_w = call(
        weights_kernel,
        "weights",
        (shape(D, 2 * PAD), shape(D, 2 * PAD), shape(D, D)),
        (ids, *pieces),
    )

    out_w, xhat = tie(out_w, xhat)
    vecs = packet[:, VEC_AT : VEC_AT + 4].astype(F32).transpose(1, 0, 2).reshape(4, 1, D)
    gain_one, bias_one, gain_two, bias_two = vecs[0], vecs[1], vecs[2], vecs[3]
    w_t_other = swap(w_t, "xh")

    mixed_own, att_rel, mlp_small, ds, keep, send, *outs = call(
        mlp_kernel,
        "mlp",
        (
            shape(128, D, dtype=F32),
            shape(512, D),
            shape(8, D, dtype=F32),
            shape(4, 128, D),
            shape(4, 2240, 128),
            shape(4, 2240, 128),
        )
        + (shape(128, D),) * 4,
        (
            ids,
            out_w,
            att,
            Part(
                packet,
                4,
                (D, 128),
                lambda ref, ids: [ref.at[2 * lax.rem(ids[ID_Z] - k + 4, 4) + ids[ID_XH], 0:D] for k in range(4)],
            ),
            gate_w,
            up_w,
            gain_two,
            bias_two,
            *dys,
            down_projection_weight,
            down_other,
        ),
        scratch=[pltpu.VMEM((2 * PAD, D), BF16), pltpu.VMEM((512, D), BF16)]
        + [pltpu.VMEM((512, 2 * PAD), BF16)] * 3
        + [pltpu.VMEM((2 * PAD, D), BF16)],
    )
    ds = exchange(ds, "z")
    mlp_chunks = (keep.astype(F32) + swap(send, "c").astype(F32)).astype(BF16)
    dmixed, blocks = call(
        norm_kernel,
        "norm_backward",
        (shape(128, D, dtype=F32), shape(8, 384, 128)),
        (ids, ds, dy_own, mixed_own, gain_two, out_w),
    )
    blocks = exchange(blocks, SHARD)

    mlp_y = mlp_chunks[0].astype(F32)
    for k in (1, 2, 3):
        mlp_y = mlp_y + turn(mlp_chunks[k], "y", -k).astype(F32)
    mlp_y = mlp_y.astype(BF16)

    grad_keep, grad_send, dq_keep, dq_send = call(
        attend_back_kernel,
        "attend_backward",
        (shape(64, 48, 128), shape(64, 48, 128), shape(512, 384), shape(1536, 128)),
        (ids, blocks, qkv_t, lse, cos, sin, xhat, w_t, gain_one, bias_one, mlp_small, att_rel),
        scratch=[
            pltpu.VMEM((SEQ, HEAD_DIM), F32),
            pltpu.VMEM((SEQ, HEAD_DIM), F32),
            pltpu.VMEM((384, SEQ), BF16),
            pltpu.VMEM((SEQ, 384), BF16),
            pltpu.VMEM((D, 384), F32),
            pltpu.VMEM((D, 256), F32),
        ],
    )

    gu_recv = exchange(mlp_y[:1536].reshape(16, 96, 128), ("z", "xh", "xl"))
    grad_send, gu_recv, w_t_other = tie(grad_send, gu_recv, w_t_other)
    chunks = (grad_keep.astype(F32) + swap(grad_send, "c").astype(F32)).astype(BF16)
    gu_piece = jnp.sum(gu_recv.reshape(4, 4, 96, 128).astype(F32), axis=1).astype(BF16).reshape(384, 128)
    do_own, do_send = mlp_y[1536:1888], mlp_y[1888:2240]
    chunks, dq_send = tie(chunks, dq_send)
    both = swap(jnp.concatenate([dq_send, do_send], axis=0), "xh")
    dq_recv = both[:1536].reshape(3, 512, 128)
    chunks = exchange(chunks, ("z", "xh", "xl", "y"))
    grad_piece = jnp.sum(chunks.reshape(8, 8, 48, 128).astype(F32), axis=1).astype(BF16).reshape(384, 128)
    do_half = (do_own.astype(F32) + both[1536:].astype(F32)).astype(BF16)
    gu_far, do_far = swap(gu_piece, "xl"), swap(do_half, "xl")
    do_piece = (do_half.astype(F32) + do_far.astype(F32)).astype(BF16)
    mlp_piece = jnp.concatenate([gu_piece, gu_far, do_piece], axis=0)
    grad_piece, mlp_piece = tie(grad_piece, mlp_piece)
    mlp_near = [mlp_piece] + [turn(mlp_piece, "y", k) for k in (1, 2, 3)]

    dfirst_part = (
        dot(dq_keep, w_t) + dot(jnp.concatenate(list(dq_recv), axis=1), w_t_other)
    ).astype(BF16)
    parts = [dfirst_part[k * 128 : k * 128 + 128] for k in range(4)]
    parts = [jnp.concatenate([outs[k], parts[k]], axis=0) for k in range(4)]
    parts = [parts[0]] + [turn(parts[k], "z", -k) for k in (1, 2, 3)]
    mine = spread(grad_piece, PLANE, 8)
    total = sum(part.astype(F32) for part in parts)
    block_output = (mixed_own + total[:128]).astype(BF16)[None]
    total = total[128:]
    normed_one, inverse_one = normalize(x_own.astype(F32))
    input_grad = (dmixed + norm_back(total * gain_one, normed_one, inverse_one)).astype(BF16)[None]

    qkv_grad, out_w_grad, qkv_bias_grad, *vectors = call(
        last_kernel,
        "last",
        (
            shape(128, 3 * D, dtype=F32),
            shape(128, D, dtype=F32),
            shape(384, dtype=F32),
        )
        + (shape(1, 128, dtype=F32),) * 4,
        (ids, mine, swap(mine, "c")),
    )
    mlp_theirs = [swap(value, "c") for value in mlp_near]
    qkv_grad, input_grad, *mlp_theirs = tie(qkv_grad, input_grad, *mlp_theirs)
    gate_up_grad, down_grad = call(
        mlp_grad_kernel,
        "mlp_grad",
        (shape(128, 2 * FF, dtype=F32), shape(UNITS, D, dtype=F32)),
        (ids, *mlp_near, *mlp_theirs),
    )
    vectors = [vector.reshape(128) for vector in vectors]

    return (
        block_output,
        input_grad,
        vectors[0],
        vectors[1],
        qkv_grad,
        qkv_bias_grad,
        out_w_grad,
        vectors[2],
        vectors[3],
        gate_up_grad,
        down_grad,
    )


def solution(mesh):
    fine = jax.sharding.Mesh(mesh.devices.reshape(2, 4, 2, 4, 2), ("xl", "y", "c", "z", "xh"))
    tokens = P(("xl", "y", "c"), SHARD, None)
    rows = P(SHARD, None)
    flat = P(SHARD)
    return jax.shard_map(
        shards,
        mesh=fine,
        in_specs=(tokens, flat, flat, rows, flat, rows, flat, flat, rows, rows, tokens),
        out_specs=(tokens, tokens, flat, flat, rows, flat, rows, flat, flat, rows, rows),
        check_vma=False,
    )
```

```python
import jax
import jax.numpy as jnp
import numpy as np
from jax import lax
from jax.experimental import pallas as pl
from jax.experimental.pallas import tpu as pltpu
from jax.sharding import PartitionSpec as P

D = 1024
HEADS = 16
HEAD_DIM = 64
FF = 2816
ROTARY = 16
SEQ = 1024
BLOCK = 256
UNITS = 352
PAD = 384

EPSILON = 1e-05
SCORE_SCALE = 0.125

SHARD = ("z", "xh")
PLANE = ("xl", "y")
F32 = jnp.float32
BF16 = jnp.bfloat16
MIB = 1024 * 1024

VEC_AT, QKV_AT, GU_AT = 1024, 1040, 1232


def normalize(values):
    center = values - jnp.mean(values, axis=-1, keepdims=True)
    variance = jnp.mean(center * center, axis=-1, keepdims=True)
    inverse = lax.rsqrt(variance + EPSILON)
    return (center * inverse, inverse)


def norm_back(scaled_grad, normed, inverse):
    return inverse * (
        scaled_grad
        - jnp.mean(scaled_grad, axis=-1, keepdims=True)
        - normed * jnp.mean(scaled_grad * normed, axis=-1, keepdims=True)
    )


def rotary_tables():
    half = ROTARY // 2
    frequency = np.float32(10000.0) ** (-np.arange(half, dtype=np.float32) * np.float32(2.0) / np.float32(ROTARY))
    angles = np.arange(SEQ, dtype=np.float32)[None, :] * frequency.astype(np.float32)[:, None]
    return np.cos(angles).astype(np.float32), np.sin(angles).astype(np.float32)


def exchange(value, axes):
    return lax.all_to_all(value, axes, 0, 0, tiled=True)


def spread(value, axes, count):
    return exchange(jnp.broadcast_to(value[None], (count,) + value.shape), axes)


def swap(value, axis):
    return lax.ppermute(value, axis, [(0, 1), (1, 0)])


def turn(value, axis, step):
    return lax.ppermute(value, axis, [(i, (i + step) % 4) for i in range(4)])


def index_of(xl, y, c, z, xh):
    return (((xl * 4 + y) * 2 + c) * 4 + z) * 2 + xh


def move(value, target):
    pairs = []
    for xl in range(2):
        for y in range(4):
            for c in range(2):
                for z in range(4):
                    for xh in range(2):
                        pairs.append((index_of(xl, y, c, z, xh), index_of(*target(xl, y, c, z, xh))))
    return lax.ppermute(value, ("xl", "y", "c", "z", "xh"), pairs)


def tie(*values):
    return lax.optimization_barrier(values)


def dot(a, b, dims=((1,), (0,))):
    return lax.dot_general(a, b, (dims, ((), ())), preferred_element_type=F32)


NT = ((1,), (1,))

ID_Y, ID_C, ID_Z, ID_XH, ID_XL = range(5)


class Part:
    def __init__(self, array, count, dims, views):
        self.array, self.shape, self.dtype, self.views = array, (count,) + dims, array.dtype, views


class Later:
    def __init__(self, copies, buffer):
        self.copies, self.buffer = copies, buffer

    def arrive(self, piece=None):
        for i, copy in enumerate(self.copies):
            if copy is not None and piece in (None, i):
                copy.wait()
                self.copies[i] = None
        return self.buffer

    def __getitem__(self, index):
        first = index[0] if isinstance(index, tuple) else None
        piece = first if isinstance(first, int) and len(self.copies) > 1 else None
        return self.arrive(piece)[index]


class Result:
    def __init__(self, source, target, sem):
        self.copy, self.buffer, self.sent = pltpu.make_async_copy(source, target, sem), source, False
        self.target, self.sem = target, sem

    def __setitem__(self, index, value):
        self.buffer[index] = value

    def __getitem__(self, index):
        return self.buffer[index]

    def send_rows(self, rows):
        pltpu.make_async_copy(self.buffer.at[rows], self.target.at[rows], self.sem).start()
        self.sent = True

    def send(self):
        if not self.sent:
            self.copy.start()
            self.sent = True


def call(kernel, name, out_shape, args, scratch=(), moved=1):
    count, outs, own = len(args) - 1, len(out_shape), len(scratch)

    def body(ids, *refs):
        sources, rest = refs[:count], refs[count:]
        targets, mine, rest = rest[:outs], rest[outs : outs + own], rest[outs + own :]
        buffers, results, (sems, out_sems) = rest[:count], rest[count:-2], rest[-2:]
        inputs = []
        at = 0
        for i in range(count):
            if isinstance(args[i + 1], Part):
                views = args[i + 1].views(sources[i], ids)
                copies = [
                    pltpu.make_async_copy(view, buffers[i].at[j], sems.at[at + j]) for j, view in enumerate(views)
                ]
            else:
                copies = [pltpu.make_async_copy(sources[i], buffers[i], sems.at[at])]
            at += len(copies)
            for copy in copies:
                copy.start()
            inputs.append(Later(copies, buffers[i]))
        outputs = [Result(results[i], targets[i], out_sems.at[i]) for i in range(outs)]
        kernel(ids, *inputs, *outputs, *mine)
        for value in inputs:
            value.arrive()
        for value in outputs:
            value.send()
        for value in outputs:
            value.copy.wait()

    flights = sum(a.shape[0] if isinstance(a, Part) else 1 for a in args[1:])
    return pl.pallas_call(
        body,
        out_shape=out_shape,
        in_specs=[pl.BlockSpec(memory_space=pltpu.SMEM)] + [pl.BlockSpec(memory_space=pltpu.HBM)] * count,
        out_specs=tuple(pl.BlockSpec(memory_space=pltpu.HBM) for _ in out_shape),
        scratch_shapes=list(scratch)
        + [pltpu.VMEM(a.shape, a.dtype) for a in list(args[1:]) + list(out_shape)]
        + [pltpu.SemaphoreType.DMA((flights,)), pltpu.SemaphoreType.DMA((outs,))],
        compiler_params=pltpu.CompilerParams(vmem_limit_bytes=60 * MIB),
        cost_estimate=pl.CostEstimate(flops=0, bytes_accessed=moved, transcendentals=0),
        name=name,
    )(*[a.array if isinstance(a, Part) else a for a in args])


def shape(*dims, dtype=BF16):
    return jax.ShapeDtypeStruct(dims, dtype)


def turned(value, cos, sin, sign):
    a = value[0:8]
    b = value[8:16]
    return jnp.concatenate([a * cos - sign * (b * sin), b * cos + sign * (a * sin), value[16:]], axis=0)


def qkv_weights(c, cols, other, w_rows, w_out):
    mine = pl.multiple_of(c * 64, 64)
    theirs = pl.multiple_of((1 - c) * 64, 64)
    for src in range(8):
        for kind in range(3):
            lanes = slice(kind * 128, kind * 128 + 128)
            at = kind * 64
            w_rows[pl.ds(src * 128 + mine, 64), lanes] = cols[0, src, at : at + 64, :]
            w_rows[pl.ds(src * 128 + theirs, 64), lanes] = other[src, kind * 64 : kind * 64 + 64, :]
    for kind in range(3):
        for src in range(8):
            w_out[kind * 128 : kind * 128 + 128, src * 128 : src * 128 + 128] = w_rows[
                src * 128 : src * 128 + 128, kind * 128 : kind * 128 + 128
            ].T


def normed_kernel(ids, packet, xhat_out):
    for block in range(8):
        x = jnp.concatenate([packet[block, cb * 128 : cb * 128 + 128, :].astype(F32) for cb in range(8)], axis=1)
        xhat_out[block * 128 : block * 128 + 128, :] = normalize(x)[0].astype(BF16)
        xhat_out.send_rows(slice(block * 128, block * 128 + 128))


def attend_kernel(ids, cols, other, packet, cos_ref, sin_ref, qkv_out, attended, lse_out, w_out, w_rows):
    c = ids[ID_C]
    s = ids[ID_Z] * 2 + ids[ID_XH]
    qkv_weights(c, cols, other, w_rows, w_out)
    w_out.send()
    vec = [packet[src, VEC_AT : VEC_AT + 16, :].astype(F32) for src in range(8)]
    gain = jnp.concatenate([v[0:1] for v in vec], axis=1)
    bias = jnp.concatenate([v[1:2] for v in vec], axis=1)
    row = lax.broadcasted_iota(jnp.int32, (16, 128), 0)
    qkv_bias = []
    for kind in range(3):
        total = jnp.zeros((16, 128), F32)
        for src in range(8):
            total += jnp.where((row >= 4) & (row < 7) & (row - 4 + 3 * src == 8 * kind + s), vec[src], 0.0)
        line = jnp.sum(total, axis=0, keepdims=True)
        qkv_bias.append(jnp.broadcast_to(line, (128, 128)).T)
    qkv_bias = jnp.concatenate(qkv_bias, axis=0)
    qkv_bias = jnp.concatenate([qkv_bias, qkv_bias], axis=1)
    for block in range(SEQ // BLOCK):
        lo = block * BLOCK
        x = jnp.concatenate(
            [
                jnp.concatenate(
                    [packet[2 * block + i, cb * 128 : cb * 128 + 128, :].astype(F32) for cb in range(8)], axis=1
                )
                for i in range(2)
            ],
            axis=0,
        )
        normed, _ = normalize(x)
        first_in = (normed * gain + bias).astype(BF16)
        part = dot(w_out[...], first_in, NT) + qkv_bias
        cos = cos_ref[:, lo : lo + BLOCK]
        sin = sin_ref[:, lo : lo + BLOCK]
        for kind in range(3):
            for head in range(2):
                base = kind * 128 + head * 64
                full = part[base : base + 64]
                if kind < 2:
                    full = turned(full, cos, sin, 1.0)
                qkv_out[base : base + 64, lo : lo + BLOCK] = full.astype(BF16)
    qkv_out.send()
    row = lax.broadcasted_iota(jnp.int32, (BLOCK, BLOCK), 0)
    col = lax.broadcasted_iota(jnp.int32, (BLOCK, BLOCK), 1)
    lse_out[...] = jnp.zeros((8, SEQ), F32)
    for block in range(SEQ // BLOCK):
        lo = block * BLOCK
        hi = lo + BLOCK
        both = []
        for head in range(2):
            keys = qkv_out[128 + head * 64 : 128 + head * 64 + 64, :hi].T
            value_t = qkv_out[256 + head * 64 : 256 + head * 64 + 64, :hi]
            query_t = qkv_out[head * 64 : head * 64 + 64, lo:hi] * jnp.bfloat16(SCORE_SCALE)
            parts = []
            if block:
                parts.append(dot(keys[:lo], query_t))
            parts.append(jnp.where(row <= col, dot(keys[lo:hi], query_t), -jnp.inf))
            scores = jnp.concatenate(parts, axis=0) if block else parts[0]
            top = jnp.max(scores, axis=0, keepdims=True)
            exps = jnp.exp(scores - top)
            total = jnp.sum(exps, axis=0, keepdims=True)
            both.append(dot(value_t, exps.astype(BF16)) / total)
            lse_out[head : head + 1, lo:hi] = top + jnp.log(total)
        out = jnp.concatenate(both, axis=0).T.astype(BF16)
        for parity in range(2):
            for zt in range(4):
                attended[2 * zt + parity, block * 128 : block * 128 + 128, :] = out[parity * 128 : parity * 128 + 128]


def weights_kernel(ids, p0, p1, p2, p3, p4, p5, p6, p7, gate_w, up_w, out_w):
    y, c = ids[ID_Y], ids[ID_C]
    for target, first, tiles in ((out_w, 192, 4), (gate_w, 0, 3), (up_w, 96, 3)):
        for k, refs in enumerate(((p0, p4), (p1, p5), (p2, p6), (p3, p7))):
            at = pl.multiple_of(lax.rem(y - k + 4, 4) * 32, 32)
            for core, ref in enumerate(refs):
                half = c if core == 0 else 1 - c
                start = half * 512 if tiles == 4 else core * PAD
                for src in range(8):
                    for cb in range(tiles):
                        lanes = pl.ds(pl.multiple_of(start + cb * 128, 128), 128)
                        rows = slice(first + cb * 32, first + cb * 32 + 32)
                        target[pl.ds(src * 128 + at, 32), lanes] = ref[src, rows, :]
        target.send()


def assemble_down(ids, own, other, down_w):
    swapped = jnp.where(ids[ID_XH] == ids[ID_C], 0, PAD)
    down_w[pl.ds(pl.multiple_of(swapped, 128), UNITS), :] = own[...]
    down_w[pl.ds(pl.multiple_of(PAD - swapped, 128), UNITS), :] = other[...]
    for base in (UNITS, PAD + UNITS):
        down_w[base : base + PAD - UNITS, :] = jnp.zeros((PAD - UNITS, D), BF16)


def cotangent(parts):
    return jnp.concatenate([part[...] for part in parts], axis=0)


def mlp_kernel(
    ids, out_w, att, x_ref, gate_w, up_w, gain_ref, bias_ref, dy0, dy1, dy2, dy3, down_own, down_other, mixed_own, att_out, small, ds, keep, send, out0, out1, out2, out3, down_w, second_out, hidden_out, dgate_out, dup_out, held
):
    z = ids[ID_Z]
    x_ref.arrive()
    gain = gain_ref[...]
    bias = bias_ref[...]
    gain_sum = jnp.zeros((1, D), F32)
    bias_sum = jnp.zeros((1, D), F32)
    for pair in range(2):
        rows = slice(pair * 256, pair * 256 + 256)
        a_parts = []
        x_parts = []
        for k in (2 * pair, 2 * pair + 1):
            place = lax.rem(z - k + 4, 4)
            at = pl.ds(pl.multiple_of(place * 128, 128), 128)
            a_parts.append(jnp.concatenate([att[src, at, :] for src in range(8)], axis=1))
            x_parts.append(
                jnp.concatenate([x_ref[k, cb * 128 : cb * 128 + 128, :] for cb in range(8)], axis=1)
            )
        attended = jnp.concatenate(a_parts, axis=0)
        att_out[rows, :] = attended
        mixed = jnp.concatenate(x_parts, axis=0).astype(F32) + dot(attended, out_w[...])
        if pair == 0:
            mixed_own[...] = mixed[:128]
        normed, _ = normalize(mixed)
        second_in = (normed * gain + bias).astype(BF16)
        second_out[rows, :] = second_in
        gate = dot(second_in, gate_w[...])
        up_part = dot(second_in, up_w[...])
        sig = jax.nn.sigmoid(gate)
        silu = gate * sig
        hidden_out[rows, :] = (silu * up_part).astype(BF16)
        dy = cotangent((dy0, dy1, dy2, dy3)[2 * pair : 2 * pair + 2])
        if pair == 0:
            assemble_down(ids, down_own, down_other, down_w)
        dhidden = dot(dy, down_w[...], NT)
        dgate = (dhidden * up_part * sig * (1.0 + gate * (1.0 - sig))).astype(BF16)
        dup = (dhidden * silu).astype(BF16)
        dgate_out[rows, :] = dgate
        dup_out[rows, :] = dup
        dsecond = dot(dgate, gate_w[...], NT) + dot(dup, up_w[...], NT)
        gain_sum += jnp.sum(dsecond * normed, axis=0, keepdims=True)
        bias_sum += jnp.sum(dsecond, axis=0, keepdims=True)
        low = dsecond.astype(BF16)
        for i in range(2):
            ds[lax.rem(z - (2 * pair + i) + 4, 4)] = low[i * 128 : i * 128 + 128]
    small[...] = jnp.concatenate([gain_sum, bias_sum, jnp.zeros((6, D), F32)], axis=0)
    ds.send()
    att_out.send()

    y, c, xh, xl = ids[ID_Y], ids[ID_C], ids[ID_XH], ids[ID_XL]

    def place(to_y):
        return lax.rem(y - to_y + 4, 4)

    for block in range(4):
        turned_in = second_out[:, block * 256 : block * 256 + 256].T
        for which, grad in ((0, dgate_out), (1, dup_out)):
            part = dot(turned_in, grad[...]).astype(BF16)
            for target, base in ((keep, 0), (send, PAD)):
                for i in range(16):
                    owner, to_xl, to_y = block * 2 + i // 8, (i // 4) % 2, i % 4
                    for cb in range(3):
                        at = (owner * 2 + to_xl) * 96 + (which * 3 + cb) * 16
                        target[place(to_y), at : at + 16, :] = part[
                            i * 16 : i * 16 + 16, base + cb * 128 : base + cb * 128 + 128
                        ]
    for target in (send, keep):
        target.send_rows((slice(None), slice(0, 1536)))
    hidden_t = hidden_out[...].T
    held[...] = dot(hidden_t, cotangent((dy0, dy1, dy2, dy3))).astype(BF16)
    for target, half in ((keep, c), (send, 1 - c)):
        for base, to_xh in ((0, c), (PAD, 1 - c)):
            for to_xl in range(2):
                rows = pl.ds(pl.multiple_of(1536 + jnp.abs(xh - to_xh) * 352 + to_xl * 176, 16), 176)
                for cb in range(4):
                    lanes = pl.ds(pl.multiple_of(half * 512 + cb * 128, 128), 128)
                    target[place(cb), rows, :] = held[base + to_xl * 176 : base + to_xl * 176 + 176, lanes]
    for target in (send, keep):
        target.send_rows((slice(None), slice(1536, 2240)))
    for pair in range(2):
        part = dot(hidden_out[pair * 256 : pair * 256 + 256, :], down_w[...]).astype(BF16)
        ((out0, out1), (out2, out3))[pair][0][...] = part[:128]
        ((out0, out1), (out2, out3))[pair][1][...] = part[128:]


def norm_kernel(ids, ds, dy, mixed_ref, gain_ref, out_w, dmixed_out, blocks):
    dsecond = ds[0].astype(F32) + ds[1].astype(F32) + ds[2].astype(F32) + ds[3].astype(F32)
    normed, inverse = normalize(mixed_ref[...])
    dmixed = dy[...].astype(F32) + norm_back(dsecond * gain_ref[...], normed, inverse)
    dmixed_out[...] = dmixed
    dproj = dmixed.astype(BF16)
    dattended = dot(dproj, out_w[...], NT).astype(BF16)
    for dest in range(8):
        blocks[dest, :128, :] = dattended[:, dest * 128 : dest * 128 + 128]
        for cb in range(2):
            at = (dest // 2) * 256 + cb * 128
            blocks[dest, 128 + cb * 128 : 256 + cb * 128, :] = dproj[:, at : at + 128]


def attend_back_kernel(
    ids, blocks, qkv, lse_ref, cos_ref, sin_ref, xhat, w_t, gain_ref, bias_ref, small, att, keep, send, dq_keep,
    dq_send, dkey, dvalue, dq_t, dq_rows, grad_rows, out_rows
):
    c, z, xh = ids[ID_C], ids[ID_Z], ids[ID_XH]
    cos = cos_ref[...]
    sin = sin_ref[...]
    row = lax.broadcasted_iota(jnp.int32, (BLOCK, BLOCK), 0)
    col = lax.broadcasted_iota(jnp.int32, (BLOCK, BLOCK), 1)
    for head in range(2):
        dkey[...] = jnp.zeros_like(dkey)
        dvalue[...] = jnp.zeros_like(dvalue)
        key_t = qkv[128 + head * 64 : 128 + head * 64 + 64, :]
        keys = key_t.T
        values = qkv[256 + head * 64 : 256 + head * 64 + 64, :].T
        dquery = []
        for block in range(SEQ // BLOCK):
            lo = block * BLOCK
            hi = lo + BLOCK
            query_t = qkv[head * 64 : head * 64 + 64, lo:hi] * jnp.bfloat16(SCORE_SCALE)
            query = query_t.T
            grad = jnp.concatenate(
                [blocks[2 * block + i, :128, head * 64 : head * 64 + 64] for i in range(2)], axis=0
            )
            grad_t = grad.T
            lse = lse_ref[head : head + 1, lo:hi]
            parts = []
            if block:
                parts.append(jnp.exp(dot(keys[:lo], query_t) - lse))
            parts.append(jnp.where(row <= col, jnp.exp(dot(keys[lo:hi], query_t) - lse), 0.0))
            shares = jnp.concatenate(parts, axis=0) if block else parts[0]
            dshares = dot(values[:hi], grad_t)
            row_dot = jnp.sum(shares * dshares, axis=0, keepdims=True)
            dscores = (shares * (dshares - row_dot)).astype(BF16)
            dvalue[:hi] += dot(shares.astype(BF16), grad)
            dkey[:hi] += dot(dscores, query)
            dquery.append(dot(key_t[:, :hi], dscores) * SCORE_SCALE)
        dquery_t = jnp.concatenate(dquery, axis=1)
        dq_t[head * 64 : head * 64 + 64, :] = turned(dquery_t, cos, sin, -1.0).astype(BF16)
        dq_t[128 + head * 64 : 128 + head * 64 + 64, :] = turned(dkey[...].T, cos, sin, -1.0).astype(BF16)
        dq_t[256 + head * 64 : 256 + head * 64 + 64, :] = dvalue[...].T.astype(BF16)
    whole = dq_t[...]
    sums = jnp.sum(whole.astype(F32), axis=1, keepdims=True)
    product = dot(whole, xhat[...])
    weights = w_t[...].astype(F32)
    gain_part = jnp.sum(product * weights, axis=0, keepdims=True)
    bias_part = jnp.sum(sums * weights, axis=0, keepdims=True)
    grad_rows[...] = (product * gain_ref[...] + sums * bias_ref[...]).T
    dproj = jnp.concatenate(
        [
            jnp.concatenate(
                [blocks[2 * lax.rem(z - k + 4, 4) + xh, 128 + cb * 128 : 256 + cb * 128, :] for cb in range(2)], axis=1
            )
            for k in range(4)
        ],
        axis=0,
    )
    for block in range(4):
        rows = slice(block * 256, block * 256 + 256)
        out_rows[rows, :] = dot(att[:, rows].T, dproj)
    lines = [
        jnp.broadcast_to(sums[kind * 128 : kind * 128 + 128], (128, 128)).T[0:1] for kind in range(3)
    ]
    filler = jnp.zeros((7, 128), F32)
    for dest in range(8):
        lanes = slice(dest * 128, dest * 128 + 128)
        lines_here = [gain_part[:, lanes], bias_part[:, lanes], small[0:1, lanes], small[1:2, lanes]] + lines
        lines_here.append(jnp.zeros((1, 128), F32))
        for e in range(8):
            tail = jnp.concatenate([lines_here[e], filler], axis=0)
            for target, half in ((keep, c), (send, 1 - c)):
                rows = pl.ds(pl.multiple_of(dest * 128 + half * 64 + e * 8, 8), 8)
                target[dest * 8 + e] = jnp.concatenate(
                    [grad_rows[rows, kind * 128 : kind * 128 + 128] for kind in range(3)]
                    + [out_rows[rows, cb * 128 : cb * 128 + 128] for cb in range(2)]
                    + [tail],
                    axis=0,
                ).astype(BF16)
    keep.send()
    send.send()
    dq_rows[...] = whole.T
    for k in range(4):
        base = lax.rem(z - k + 4, 4) * 256
        dq_keep[k * 128 : k * 128 + 128, :] = dq_rows[pl.ds(pl.multiple_of(base + xh * 128, 128), 128), :]
        theirs = pl.ds(pl.multiple_of(base + (1 - xh) * 128, 128), 128)
        for kind in range(3):
            at = kind * 512 + k * 128
            dq_send[at : at + 128, :] = dq_rows[theirs, kind * 128 : kind * 128 + 128]


def mlp_grad_kernel(ids, m0, m1, m2, m3, o0, o1, o2, o3, gate_up, down):
    c, y, xl = ids[ID_C], ids[ID_Y], ids[ID_XL]
    mine, other = (m0, m1, m2, m3), (o0, o1, o2, o3)
    zero = c == 0

    def place(k, i):
        return lax.rem(xl + i, 2), lax.rem(y - k + 4, 4)

    def wide(ref, i, z, which):
        at = i * 384 + z * 96 + which * 48
        return jnp.concatenate(
            [ref[at + cb * 16 : at + cb * 16 + 16, :].astype(F32) for cb in range(3)], axis=1
        )[:, :UNITS]

    for k in range(4):
        for i in range(2):
            to_xl, to_y = place(k, i)
            rows = pl.ds(pl.multiple_of(to_xl * 64 + to_y * 16, 16), 16)
            for which in range(2):
                parts = []
                for z in range(4):
                    a, b = wide(mine[k], i, z, which), wide(other[k], i, z, which)
                    parts += [jnp.where(zero, a, b), jnp.where(zero, b, a)]
                gate_up[rows, which * FF : which * FF + FF] = jnp.concatenate(parts, axis=1)
            gate_up.send_rows(rows)
    for refs, half in ((mine, c), (other, 1 - c)):
        for k in range(4):
            lanes = pl.ds(pl.multiple_of(half * 512 + place(k, 0)[1] * 128, 128), 128)
            down[:, lanes] = refs[k][768:1120, :].astype(F32)


def last_kernel(ids, mine, other, qkv, out_w, qkv_bias, attn_gain, attn_bias, mlp_gain, mlp_bias):
    c = ids[ID_C]
    s = ids[ID_Z] * 2 + ids[ID_XH]
    totals = []
    for ref, half in ((mine, c), (other, 1 - c)):
        for e in range(8):
            rows = pl.ds(pl.multiple_of(half * 64 + e * 8, 8), 8)
            tiles = [ref[e, src * 48 : src * 48 + 48, :].astype(F32) for src in range(8)]
            for src in range(8):
                for kind in range(3):
                    lanes = slice(kind * D + src * 128, kind * D + src * 128 + 128)
                    qkv[rows, lanes] = tiles[src][kind * 8 : kind * 8 + 8]
            for z in range(4):
                for cb in range(2):
                    lanes = slice(z * 256 + cb * 128, z * 256 + cb * 128 + 128)
                    at = slice(24 + cb * 8, 32 + cb * 8)
                    out_w[rows, lanes] = tiles[2 * z][at] + tiles[2 * z + 1][at]
            if ref is mine:
                totals.append([tile[40:41] for tile in tiles])
    for e, vector in enumerate((attn_gain, attn_bias, mlp_gain, mlp_bias)):
        total = totals[e][0]
        for line in totals[e][1:]:
            total = total + line
        vector[...] = total
    for i in range(3):
        block = 3 * s + i
        found = jnp.zeros((1, 128), F32)
        for src in range(8):
            for kind in range(3):
                found += jnp.where(block == 8 * kind + src, totals[4 + kind][src], 0.0)
        qkv_bias[i * 128 : i * 128 + 128] = found.reshape(128)


def shards(
    block_input,
    attn_gain,
    attn_bias,
    query_key_value_weight,
    query_key_value_bias,
    output_projection_weight,
    mlp_gain,
    mlp_bias,
    gate_up_projection_weight,
    down_projection_weight,
    out_grad,
):
    y = lax.axis_index("y")
    c = lax.axis_index("c")
    z = lax.axis_index("z")
    xh = lax.axis_index("xh")
    xl = lax.axis_index("xl")
    ids = jnp.stack([y, c, z, xh, xl]).astype(jnp.int32)
    x_own = block_input[0]
    dy_own = out_grad[0]
    cos_np, sin_np = rotary_tables()
    cos, sin = jnp.asarray(cos_np), jnp.asarray(sin_np)

    gu_rows = lax.dynamic_slice_in_dim(gate_up_projection_weight, y * 32, 32, 0).reshape(32, 2, 4, 2, UNITS)
    gu_rows = lax.dynamic_index_in_dim(gu_rows, c, 3, keepdims=False)
    gu_rows = jnp.pad(gu_rows, ((0, 0), (0, 0), (0, 0), (0, PAD - UNITS))).reshape(32, 2, 4, 3, 128)
    gu_part = jnp.broadcast_to(gu_rows.transpose(2, 1, 3, 0, 4).reshape(4, 1, 192, 128), (4, 2, 192, 128))
    out_rows = lax.dynamic_slice(output_projection_weight, (y * 32, c * 512), (32, 512))
    out_part = out_rows.reshape(32, 4, 128).transpose(1, 0, 2).reshape(128, 128)
    tail = jnp.broadcast_to(out_part[None], (8, 128, 128))

    x_part = x_own.reshape(128, 8, 128).transpose(1, 0, 2).reshape(D, 128)
    vec = jnp.concatenate(
        [
            jnp.stack([attn_gain, attn_bias, mlp_gain, mlp_bias]),
            query_key_value_bias.reshape(3, 128),
            jnp.zeros((9, 128), BF16),
        ]
    )
    qkv_rows = lax.dynamic_slice_in_dim(query_key_value_weight, c * 64, 64, 0)
    qkv_part = qkv_rows.reshape(64, 3, 8, 128).transpose(2, 1, 0, 3).reshape(8, 192, 128)
    head = jnp.broadcast_to(jnp.concatenate([x_part, vec])[None], (8, QKV_AT, 128))
    packet = jnp.concatenate([head, qkv_part, gu_part.reshape(8, 192, 128), tail], axis=1)
    packet, down_now = tie(exchange(packet, SHARD), down_projection_weight)
    down_other = swap(down_now, "xh")
    piece = packet[:, GU_AT:]
    before, after = turn(piece, "y", 1), turn(piece, "y", 3)
    qkv_other = swap(packet[:, QKV_AT:GU_AT], "c")
    cols = Part(packet, 1, (8, GU_AT - QKV_AT, 128), lambda ref, ids: [ref.at[:, QKV_AT:GU_AT]])
    tokens = Part(packet, 8, (QKV_AT, 128), lambda ref, ids: [ref.at[i, 0:QKV_AT] for i in range(8)])
    qkv_t, att_blocks, lse, w_t = call(
        attend_kernel,
        "attend_forward",
        (shape(384, SEQ), shape(8, 512, 128), shape(8, SEQ, dtype=F32), shape(384, D)),
        (ids, cols, qkv_other, tokens, cos, sin),
        scratch=[pltpu.VMEM((D, 384), BF16)],
    )
    att_blocks, packet_late, dy_now, far = tie(att_blocks, packet, dy_own, piece)
    att = exchange(att_blocks, SHARD)
    dy_now, before, after, down_other = tie(dy_now, before, after, down_other)
    dys = [dy_now] + [turn(dy_now, "z", k) for k in (1, 2, 3)]
    pieces = [piece, before, turn(far, "y", 2), after]
    (xhat,) = call(
        normed_kernel,
        "normed_input",
        (shape(SEQ, D),),
        (ids, Part(packet_late, 8, (D, 128), lambda ref, ids: [ref.at[i, 0:D] for i in range(8)])),
    )
    pieces += [swap(p, "c") for p in pieces]
    gate_w, up_w, out_w = call(
        weights_kernel,
        "weights",
        (shape(D, 2 * PAD), shape(D, 2 * PAD), shape(D, D)),
        (ids, *pieces),
    )

    out_w, xhat = tie(out_w, xhat)
    vecs = packet[:, VEC_AT : VEC_AT + 4].astype(F32).transpose(1, 0, 2).reshape(4, 1, D)
    gain_one, bias_one, gain_two, bias_two = vecs[0], vecs[1], vecs[2], vecs[3]
    w_t_other = swap(w_t, "xh")

    mixed_own, att_rel, mlp_small, ds, keep, send, *outs = call(
        mlp_kernel,
        "mlp",
        (
            shape(128, D, dtype=F32),
            shape(512, D),
            shape(8, D, dtype=F32),
            shape(4, 128, D),
            shape(4, 2240, 128),
            shape(4, 2240, 128),
        )
        + (shape(128, D),) * 4,
        (
            ids,
            out_w,
            att,
            Part(
                packet,
                4,
                (D, 128),
                lambda ref, ids: [ref.at[2 * lax.rem(ids[ID_Z] - k + 4, 4) + ids[ID_XH], 0:D] for k in range(4)],
            ),
            gate_w,
            up_w,
            gain_two,
            bias_two,
            *dys,
            down_projection_weight,
            down_other,
        ),
        scratch=[pltpu.VMEM((2 * PAD, D), BF16), pltpu.VMEM((512, D), BF16)]
        + [pltpu.VMEM((512, 2 * PAD), BF16)] * 3
        + [pltpu.VMEM((2 * PAD, D), BF16)],
    )
    ds = exchange(ds, "z")
    mlp_chunks = (keep.astype(F32) + swap(send, "c").astype(F32)).astype(BF16)
    dmixed, blocks = call(
        norm_kernel,
        "norm_backward",
        (shape(128, D, dtype=F32), shape(8, 384, 128)),
        (ids, ds, dy_own, mixed_own, gain_two, out_w),
    )
    blocks = exchange(blocks, SHARD)

    mlp_y = mlp_chunks[0].astype(F32)
    for k in (1, 2, 3):
        mlp_y = mlp_y + turn(mlp_chunks[k], "y", -k).astype(F32)
    mlp_y = mlp_y.astype(BF16)

    grad_keep, grad_send, dq_keep, dq_send = call(
        attend_back_kernel,
        "attend_backward",
        (shape(64, 48, 128), shape(64, 48, 128), shape(512, 384), shape(1536, 128)),
        (ids, blocks, qkv_t, lse, cos, sin, xhat, w_t, gain_one, bias_one, mlp_small, att_rel),
        scratch=[
            pltpu.VMEM((SEQ, HEAD_DIM), F32),
            pltpu.VMEM((SEQ, HEAD_DIM), F32),
            pltpu.VMEM((384, SEQ), BF16),
            pltpu.VMEM((SEQ, 384), BF16),
            pltpu.VMEM((D, 384), F32),
            pltpu.VMEM((D, 256), F32),
        ],
    )

    gu_recv = exchange(mlp_y[:1536].reshape(16, 96, 128), ("z", "xh", "xl"))
    grad_send, gu_recv, w_t_other = tie(grad_send, gu_recv, w_t_other)
    chunks = (grad_keep.astype(F32) + swap(grad_send, "c").astype(F32)).astype(BF16)
    gu_piece = jnp.sum(gu_recv.reshape(4, 4, 96, 128).astype(F32), axis=1).astype(BF16).reshape(384, 128)
    do_own, do_send = mlp_y[1536:1888], mlp_y[1888:2240]
    chunks, dq_send = tie(chunks, dq_send)
    both = swap(jnp.concatenate([dq_send, do_send], axis=0), "xh")
    dq_recv = both[:1536].reshape(3, 512, 128)
    chunks = exchange(chunks, ("z", "xh", "xl", "y"))
    grad_piece = jnp.sum(chunks.reshape(8, 8, 48, 128).astype(F32), axis=1).astype(BF16).reshape(384, 128)
    do_half = (do_own.astype(F32) + both[1536:].astype(F32)).astype(BF16)
    gu_far, do_far = swap(gu_piece, "xl"), swap(do_half, "xl")
    do_piece = (do_half.astype(F32) + do_far.astype(F32)).astype(BF16)
    mlp_piece = jnp.concatenate([gu_piece, gu_far, do_piece], axis=0)
    grad_piece, mlp_piece = tie(grad_piece, mlp_piece)
    mlp_near = [mlp_piece] + [turn(mlp_piece, "y", k) for k in (1, 2, 3)]

    dfirst_part = (
        dot(dq_keep, w_t) + dot(jnp.concatenate(list(dq_recv), axis=1), w_t_other)
    ).astype(BF16)
    parts = [dfirst_part[k * 128 : k * 128 + 128] for k in range(4)]
    parts = [jnp.concatenate([outs[k], parts[k]], axis=0) for k in range(4)]
    parts = [parts[0]] + [turn(parts[k], "z", -k) for k in (1, 2, 3)]
    mine = spread(grad_piece, PLANE, 8)
    total = sum(part.astype(F32) for part in parts)
    block_output = (mixed_own + total[:128]).astype(BF16)[None]
    total = total[128:]
    normed_one, inverse_one = normalize(x_own.astype(F32))
    input_grad = (dmixed + norm_back(total * gain_one, normed_one, inverse_one)).astype(BF16)[None]

    qkv_grad, out_w_grad, qkv_bias_grad, *vectors = call(
        last_kernel,
        "last",
        (
            shape(128, 3 * D, dtype=F32),
            shape(128, D, dtype=F32),
            shape(384, dtype=F32),
        )
        + (shape(1, 128, dtype=F32),) * 4,
        (ids, mine, swap(mine, "c")),
    )
    mlp_theirs = [swap(value, "c") for value in mlp_near]
    qkv_grad, input_grad, *mlp_theirs = tie(qkv_grad, input_grad, *mlp_theirs)
    gate_up_grad, down_grad = call(
        mlp_grad_kernel,
        "mlp_grad",
        (shape(128, 2 * FF, dtype=F32), shape(UNITS, D, dtype=F32)),
        (ids, *mlp_near, *mlp_theirs),
    )
    vectors = [vector.reshape(128) for vector in vectors]

    return (
        block_output,
        input_grad,
        vectors[0],
        vectors[1],
        qkv_grad,
        qkv_bias_grad,
        out_w_grad,
        vectors[2],
        vectors[3],
        gate_up_grad,
        down_grad,
    )


def solution(mesh):
    fine = jax.sharding.Mesh(mesh.devices.reshape(2, 4, 2, 4, 2), ("xl", "y", "c", "z", "xh"))
    tokens = P(("xl", "y", "c"), SHARD, None)
    rows = P(SHARD, None)
    flat = P(SHARD)
    return jax.shard_map(
        shards,
        mesh=fine,
        in_specs=(tokens, flat, flat, rows, flat, rows, flat, flat, rows, rows, tokens),
        out_specs=(tokens, tokens, flat, flat, rows, flat, rows, flat, flat, rows, rows),
        check_vma=False,
    )
```
